32 devices in a mesh: rep: 2 (over x), node: 2 (over core), local: 8 (over z, y).
Axes of the slice: x: 2, y: 2, z: 4, core: 2. Of those that a mesh axis runs over, the one named last changes fastest.
Arguments:
- tokens: bfloat16 [4096, 3584], P(('rep', 'node', 'local')), parts along dimension 0, may hold values from -6 to 6
- grads: bfloat16 [4096, 8, 1024], P(('rep', 'node', 'local')), parts along dimension 0, may hold values from -6 to 6
- route_weights: float32 [4096, 8], P(('rep', 'node', 'local')), parts along dimension 0, may hold values from 0.1 to 1
- route_ids: int32 [4096, 8], P(('rep', 'node', 'local')), parts along dimension 0, may hold values from 0 to 1, as said below
- group_picks: int32 [4096, 4], P(('rep', 'node', 'local')), parts along dimension 0, may hold values from 0 to 7, as said below
- frozen_up: bfloat16 [16, 3584, 1024], P(('node', 'local')), may hold values from -0.09375 to 0.09375
- factor_a: bfloat16 [16, 3584, 32], P(('node', 'local')), may hold values from -0.09375 to 0.09375
- factor_b: bfloat16 [16, 32, 1024], P(('node', 'local')), may hold values from -1 to 1
Outputs:
- input_grad: bfloat16 [4096, 3584], P(('rep', 'node', 'local')), parts along dimension 0
- grad_a: float32 [32, 3584, 32], P(('rep', 'node', 'local')), parts along dimension 0
- grad_b: float32 [32, 32, 1024], P(('rep', 'node', 'local')), parts along dimension 0
The draws below stay inside these ranges and needn't reach their ends.
There are 2 independent parts, one for each index of `rep`. The reference program is written for one: setup_inputs(seed, part) draws one part's arguments, and reference() takes and returns one part's arrays. A program takes and returns all parts, laid end to end along the dimension named above; an argument that names none is the same for every part. Nothing has to cross between parts.
Inputs may be any that keep to these rules, and one draw needn't show every extreme that they name: `route_ids`: A token's 4 groups are distinct, so its 8 experts are distinct. Among the tokens of one device no expert is named by more than 80 routes; in every draw one group is picked by exactly 80 tokens of every device, and each of its 2 experts is named by exactly 80 routes of every device. The experts of one group named by one device's routes differ in their counts by at most one. `group_picks`: no group is picked by more than 80 tokens of one device.
All inputs are finite; a program needn't handle non-finite values.
Results may differ from the reference program's by a relative error of at most 0.0058.
Values may be sent and summed in bfloat16 or wider, within the bound.
A program may use at most 192 MiB of HBM per device.

```python
import math
import jax
import jax.numpy as jnp
from jax import lax

DW = 3584
FFW = 1024
RANK = 32
GROUPS = 8
GPICK = 4
TOPK = 8
TOK_DEV = 128
HOT_TOK = 80
EXPERTS = 16
GSIZE = 2
MOST = 80
TOKENS = 2048
N_NODE = 2
N_LOCAL = 8


def block_tables(key, busiest):
    rest = GPICK * TOK_DEV - HOT_TOK
    base = rest // (GROUPS - 1)
    extra = rest - base * (GROUPS - 1)
    spread = min(base, HOT_TOK - base - 1)
    key_order, key_shift, key_perm, key_groups = jax.random.split(key, 4)
    placing = jax.random.permutation(key_order, TOK_DEV).astype(jnp.int32)
    shifts = jax.random.randint(key_shift, (GROUPS - 1,), 0, spread + 1).astype(jnp.int32)
    others = base + shifts - jnp.roll(shifts, -1) + (jnp.arange(GROUPS - 1, dtype=jnp.int32) < extra).astype(jnp.int32)
    counts = jnp.concatenate([jnp.full((1,), HOT_TOK, jnp.int32), others.astype(jnp.int32)])
    ends = jnp.cumsum(counts).astype(jnp.int32)
    starts = ends - counts
    slots = jnp.arange(GPICK * TOK_DEV, dtype=jnp.int32)
    run_index = jnp.sum((slots[:, None] >= ends[None, :-1]).astype(jnp.int32), axis=1).astype(jnp.int32)
    run_rank = slots - starts[run_index]
    shuffled = jax.random.permutation(key_groups, GROUPS - 1).astype(jnp.int32)
    later = (busiest + 1 + shuffled[jnp.maximum(run_index - 1, 0)]) % GROUPS
    group_of = jnp.where(run_index == 0, busiest, later).astype(jnp.int32)
    member_keys = jax.random.split(key_perm, GROUPS)
    members = jnp.stack([jax.random.permutation(member_keys[g], GSIZE).astype(jnp.int32) for g in range(GROUPS)])
    first_pick = members[group_of, 2 * run_rank % GSIZE]
    second_pick = members[group_of, (2 * run_rank + 1) % GSIZE]
    inverse = jnp.argsort(placing).astype(jnp.int32)
    position = jnp.arange(GPICK, dtype=jnp.int32)[None, :] * TOK_DEV + inverse[:, None]
    picks = group_of[position]
    within = jnp.stack([first_pick[position], second_pick[position]], axis=2).reshape(TOK_DEV, TOPK)
    return (picks.astype(jnp.int32), within.astype(jnp.int32))


def routing_tables(key):
    device_count = N_NODE * N_LOCAL
    busiest = jax.random.randint(jax.random.fold_in(key, 11), (), 0, GROUPS).astype(jnp.int32)
    block_keys = jax.random.split(jax.random.fold_in(key, 12), device_count)
    picks, within = jax.vmap(lambda one_key: block_tables(one_key, busiest))(block_keys)
    return (picks.reshape(TOKENS, GPICK), within.reshape(TOKENS, TOPK))


def draw_group_picks(key, part):
    return routing_tables(key)[0]


def draw_route_ids(key, part):
    return routing_tables(key)[1]


def steps_of(rng, shape, pieces, low, largest):
    def one(dim, parts):
        heights = jax.random.uniform(jax.random.fold_in(jax.random.fold_in(rng, 6), dim), (parts,), jnp.float32, low / len(pieces), largest / len(pieces))
        return jnp.repeat(jnp.exp(heights), shape[dim] // parts).reshape((-1,) + (1,) * (len(shape) - dim - 1))

    gain = one(*pieces[0])
    for cut in pieces[1:]:
        gain = gain * one(*cut)
    return gain


def normal_values(key, extent, scale, limit, shards=(), kind=jnp.bfloat16):
    drawn = scale * jax.random.normal(key, extent, jnp.float32)
    if shards:
        drawn = drawn * steps_of(key, extent, shards, -0.22, 0.18)
    return jnp.clip(drawn, -limit, limit).astype(kind)


def setup_inputs(seed: int = 0, part: int = 0) -> dict:
    arg_keys = jax.random.split(jax.random.key(seed), 9)
    own_keys = jax.random.split(jax.random.fold_in(arg_keys[8], part), 9)
    tokens = normal_values(own_keys[0], (TOKENS, DW), 1.0, 6.0, ((0, 16),))
    grads = normal_values(own_keys[1], (TOKENS, TOPK, FFW), 1.0, 6.0, ((0, 16),))
    route_weights = jnp.clip(jnp.exp(math.log(1.0) - 2.3025851 * jax.random.uniform(own_keys[2], (TOKENS, TOPK), jnp.float32) ** steps_of(own_keys[2], (TOKENS, TOPK), ((0, 16),), -0.2, 0.2)), 0.1, 1.0)
    route_ids = draw_route_ids(jax.random.fold_in(jax.random.fold_in(arg_keys[8], part), 71), part)
    group_picks = draw_group_picks(jax.random.fold_in(jax.random.fold_in(arg_keys[8], part), 71), part)
    frozen_up = normal_values(arg_keys[5], (EXPERTS, DW, FFW), DW ** -0.5, 0.09375, ((0, 16),))
    factor_a = normal_values(arg_keys[6], (EXPERTS, DW, RANK), DW ** -0.5, 0.09375, ((0, 16),))
    factor_b = normal_values(arg_keys[7], (EXPERTS, RANK, FFW), RANK ** -0.5, 1.0, ((0, 16),))
    return dict(tokens=tokens, grads=grads, route_weights=route_weights, route_ids=route_ids, group_picks=group_picks, frozen_up=frozen_up, factor_a=factor_a, factor_b=factor_b)


adapter_scale_factor = 0.25
weight_gradient_total = 1.0 / 32.0


def reference(tokens, grads, route_weights, route_ids, group_picks, frozen_up, factor_a, factor_b):
    tok_total = tokens.shape[0]
    picks = jnp.repeat(group_picks, 2, axis=1)
    experts = (picks * GSIZE + route_ids).reshape(-1).astype(jnp.int32)
    pair_count = experts.shape[0]
    scaled = (grads.astype(jnp.float32) * route_weights[:, :, None]).astype(jnp.bfloat16)
    scaled = scaled.reshape(pair_count, FFW)
    scaled_pad = jnp.concatenate([scaled, jnp.zeros((1, FFW), jnp.bfloat16)], axis=0)
    tokens_pad = jnp.concatenate([tokens, jnp.zeros((1, DW), jnp.bfloat16)], axis=0)
    capacity = N_NODE * N_LOCAL * MOST

    def one_expert(total, expert):
        picked = jnp.nonzero(experts == expert, size=capacity, fill_value=pair_count)[0].astype(jnp.int32)
        owner = jnp.where(picked < pair_count, picked // TOPK, tok_total).astype(jnp.int32)
        input_rows = tokens_pad[owner]
        gradient_rows = scaled_pad[picked]
        frozen = frozen_up[expert]
        first = factor_a[expert]
        second = factor_b[expert]
        rank_space_rows = jnp.dot(gradient_rows, second.T, preferred_element_type=jnp.float32).astype(jnp.bfloat16)
        dense_product = jnp.dot(gradient_rows, frozen.T, preferred_element_type=jnp.float32)
        low_rank_product = jnp.dot(rank_space_rows, first.T, preferred_element_type=jnp.float32)
        route_gradient = (dense_product + adapter_scale_factor * low_rank_product).astype(jnp.bfloat16)
        projected_rows = jnp.dot(input_rows, first, preferred_element_type=jnp.float32).astype(jnp.bfloat16)
        first_factor_gradient = weight_gradient_total * adapter_scale_factor * jnp.dot(input_rows.T, rank_space_rows, preferred_element_type=jnp.float32)
        second_factor_gradient = weight_gradient_total * adapter_scale_factor * jnp.dot(projected_rows.T, gradient_rows, preferred_element_type=jnp.float32)
        total = total.at[owner].add(route_gradient.astype(jnp.float32), mode="drop")
        return total, (first_factor_gradient, second_factor_gradient)

    start = jnp.zeros((tok_total, DW), jnp.float32)
    total, (grad_a, grad_b) = lax.scan(one_expert, start, jnp.arange(EXPERTS, dtype=jnp.int32))
    return total.astype(jnp.bfloat16), grad_a, grad_b
```

```python
import jax
import jax.numpy as jnp
from jax import lax
from jax.sharding import PartitionSpec as P

GROUPS = 8


adapter_scale_factor = 0.25
weight_gradient_total = 1.0 / 32.0


def slot_ranks(expert_flat, device_count):
    onehot = (expert_flat[:, None] == jnp.arange(device_count, dtype=jnp.int32)[None, :]).astype(
        jnp.int32
    )
    earlier = jnp.cumsum(onehot, axis=0) - onehot
    return jnp.sum(earlier * onehot, axis=1)


def slot_grads(arrived, arrived_grads, frozen, first, second):
    lead = arrived.shape[:-1]
    input_rows = arrived.reshape(-1, arrived.shape[-1])
    gradient_rows = arrived_grads.reshape(-1, arrived_grads.shape[-1])
    rank_space_rows = lax.dot_general(
        gradient_rows, second, (((1,), (1,)), ((), ())), preferred_element_type=jnp.float32
    ).astype(jnp.bfloat16)
    joined_rows = jnp.concatenate([gradient_rows, rank_space_rows], axis=1)
    joined_weight = jnp.concatenate([frozen, first * adapter_scale_factor], axis=1)
    route_gradient = lax.dot_general(
        joined_rows, joined_weight, (((1,), (1,)), ((), ())), preferred_element_type=jnp.float32
    ).astype(jnp.bfloat16)
    projected_rows = jnp.dot(input_rows, first, preferred_element_type=jnp.float32).astype(
        jnp.bfloat16
    )
    return (
        route_gradient.reshape(lead + (frozen.shape[0],)),
        rank_space_rows.reshape(lead + (second.shape[0],)),
        projected_rows.reshape(lead + (second.shape[0],)),
    )


def send_buffers(tokens, scaled, target, device_count, slot_most):
    tok_rows, width = tokens.shape
    pair_count, hidden = scaled.shape
    topk = pair_count // tok_rows
    scaled_pad = jnp.concatenate([scaled, jnp.zeros((1, hidden), jnp.bfloat16)], axis=0)
    tokens_pad = jnp.concatenate([tokens, jnp.zeros((1, width), jnp.bfloat16)], axis=0)
    source = jnp.full((device_count * slot_most,), pair_count, jnp.int32)
    source = source.at[target].set(jnp.arange(pair_count, dtype=jnp.int32))
    owner = jnp.where(source < pair_count, source // topk, tok_rows)
    send_x = tokens_pad[owner].reshape(device_count, slot_most, width)
    send_g = scaled_pad[source].reshape(device_count, slot_most, hidden)
    return (send_x, send_g)


def sparse_body(tokens, grads, route_weights, route_ids, group_picks, frozen_up, factor_a, factor_b):
    tok_rows = tokens.shape[0]
    topk = route_ids.shape[1]
    width = tokens.shape[1]
    hidden = grads.shape[2]
    node_count = lax.axis_size("node")
    local_count = lax.axis_size("local")
    device_count = node_count * local_count
    group_size = device_count // GROUPS
    slot_most = 2 * (5 * tok_rows // 8) // group_size
    pair_count = tok_rows * topk
    frozen = frozen_up[0]
    first = factor_a[0]
    second = factor_b[0]
    experts = jnp.repeat(group_picks, 2, axis=1) * group_size + route_ids
    expert_flat = experts.reshape(-1)
    ranks = slot_ranks(expert_flat, device_count)
    target = expert_flat * slot_most + ranks
    scaled = (
        (grads.astype(jnp.float32) * route_weights[:, :, None])
        .astype(jnp.bfloat16)
        .reshape(pair_count, hidden)
    )
    send_x, send_g = send_buffers(tokens, scaled, target, device_count, slot_most)
    pieces = (
        lax.all_to_all(send_x, ("node", "local"), split_axis=0, concat_axis=0, tiled=True),
        lax.all_to_all(send_g, ("node", "local"), split_axis=0, concat_axis=0, tiled=True),
    )
    route_gradient, rank_space_rows, projected_rows = slot_grads(
        pieces[0], pieces[1], frozen, first, second
    )
    arrived, arrived_grads, route_gradient, rank_space_rows, projected_rows = (
        pieces[0],
        pieces[1],
        route_gradient,
        rank_space_rows,
        projected_rows,
    )
    input_rows = arrived.reshape(-1, width)
    gradient_rows = arrived_grads.reshape(-1, hidden)
    first_factor_gradient = (
        weight_gradient_total
        * adapter_scale_factor
        * lax.dot_general(
            input_rows,
            rank_space_rows.reshape(-1, rank_space_rows.shape[-1]),
            (((0,), (0,)), ((), ())),
            preferred_element_type=jnp.float32,
        )
    )
    second_factor_gradient = (
        weight_gradient_total
        * adapter_scale_factor
        * lax.dot_general(
            projected_rows.reshape(-1, projected_rows.shape[-1]),
            gradient_rows,
            (((0,), (0,)), ((), ())),
            preferred_element_type=jnp.float32,
        )
    )
    returned = lax.all_to_all(
        route_gradient, ("node", "local"), split_axis=0, concat_axis=0, tiled=True
    )
    picked = returned.reshape(-1, width)[target]
    input_grad = jnp.sum(picked.reshape(tok_rows, topk, width).astype(jnp.float32), axis=1).astype(
        jnp.bfloat16
    )
    return (input_grad, first_factor_gradient[None], second_factor_gradient[None])


def scale_routes(grads, route_weights):
    pair_count = grads.shape[0] * grads.shape[1]
    return (
        (grads.astype(jnp.float32) * route_weights[:, :, None])
        .astype(jnp.bfloat16)
        .reshape(pair_count, grads.shape[2])
    )


def dense_body(tokens, grads, route_weights, route_ids, group_picks, frozen_up, factor_a, factor_b):
    tok_rows, width = tokens.shape
    topk = route_ids.shape[1]
    hidden = grads.shape[2]
    rank = factor_b.shape[1]
    axes = ("node", "local")
    device_count = lax.axis_size("node") * lax.axis_size("local")
    me = lax.axis_index("node") * lax.axis_size("local") + lax.axis_index("local")
    group_size = device_count // GROUPS
    slot_most = 2 * (5 * tok_rows // 8) // group_size
    f32, bf16 = jnp.float32, jnp.bfloat16
    experts = jnp.repeat(group_picks, 2, axis=1) * group_size + route_ids
    expert_flat = experts.reshape(-1)
    first_t = factor_a[0].T
    second = factor_b[0]
    table = jnp.zeros((rank, tok_rows), bf16).at[:topk].set(experts.T.astype(bf16))
    shared = lax.all_gather(
        jnp.concatenate([first_t, second, table], axis=1), axes, axis=0, tiled=True
    )
    all_first = shared[:, :width]
    all_second = shared[:, width : width + hidden]
    tables = shared[:, width + hidden :].reshape(device_count, rank, tok_rows)[:, :topk]

    ids = jnp.arange(device_count, dtype=jnp.int32)
    member = (experts[:, :, None] == ids[None, None, :]).any(axis=1)
    order = jnp.cumsum(member.astype(jnp.int32), axis=0) - 1
    ranks = jnp.sum(jnp.where(experts[:, :, None] == ids, order[:, None, :], 0), axis=2)
    target = experts * slot_most + ranks
    scaled = scale_routes(grads, route_weights)
    slots = jnp.arange(device_count * slot_most, dtype=jnp.int32)
    pack = (target.reshape(1, -1) == slots[:, None]).astype(bf16)
    send_g = jnp.dot(pack, scaled, preferred_element_type=f32).astype(bf16)
    arrived = lax.all_to_all(
        send_g.reshape(device_count, slot_most, hidden), axes, split_axis=0, concat_axis=0, tiled=True
    )

    owner_mask = expert_flat[:, None] == jnp.repeat(ids, rank)[None, :]
    middle = lax.dot_general(scaled, all_second, (((1,), (1,)), ((), ())), preferred_element_type=f32)
    middle = jnp.where(owner_mask, middle, 0.0).reshape(tok_rows, topk, -1).sum(axis=1).astype(bf16)
    projected = lax.dot_general(
        tokens, all_first, (((1,), (1,)), ((), ())), preferred_element_type=f32
    ).astype(bf16)
    projected = jnp.where(
        owner_mask.reshape(tok_rows, topk, -1), projected[:, None, :], jnp.zeros((), bf16)
    ).reshape(tok_rows * topk, -1)
    share_a = lax.dot_general(middle, tokens, (((0,), (0,)), ((), ())), preferred_element_type=f32)
    share_b = lax.dot_general(projected, scaled, (((0,), (0,)), ((), ())), preferred_element_type=f32)
    shares = jnp.concatenate([share_a.astype(bf16), share_b.astype(bf16)], axis=1)
    factor_gradients = lax.psum_scatter(shares, "node", scatter_dimension=0, tiled=True)
    factor_gradients = lax.psum_scatter(factor_gradients, "local", scatter_dimension=0, tiled=True)
    factor_gradients = factor_gradients.astype(f32) * (weight_gradient_total * adapter_scale_factor)

    mine = (tables == me.astype(bf16)).any(axis=1)
    place = jnp.cumsum(mine.astype(jnp.int32), axis=1) - 1
    unpack = (
        mine[:, :, None] & (place[:, :, None] == jnp.arange(slot_most, dtype=jnp.int32))
    ).astype(bf16)
    rows = (
        lax.dot_general(unpack, arrived, (((2,), (1,)), ((0,), (0,))), preferred_element_type=f32)
        .astype(bf16)
        .reshape(device_count * tok_rows, hidden)
    )
    row_middle = lax.dot_general(
        rows, second, (((1,), (1,)), ((), ())), preferred_element_type=f32
    ).astype(bf16)
    joined_rows = jnp.concatenate([rows, row_middle], axis=1)
    joined_weight = jnp.concatenate([frozen_up[0], factor_a[0] * adapter_scale_factor], axis=1)
    partial = lax.dot_general(
        joined_rows, joined_weight, (((1,), (1,)), ((), ())), preferred_element_type=f32
    ).astype(bf16)
    partial = lax.psum_scatter(partial, "node", scatter_dimension=0, tiled=True)
    input_grad = lax.psum_scatter(partial, "local", scatter_dimension=0, tiled=True)
    return (input_grad, factor_gradients[:, :width].T[None], factor_gradients[:, width:][None])


def body(tokens, grads, route_weights, route_ids, group_picks, frozen_up, factor_a, factor_b):
    tok_rows = tokens.shape[0]
    group_size = lax.axis_size("node") * lax.axis_size("local") // GROUPS
    slot_most = 2 * (5 * tok_rows // 8) // group_size
    plan = dense_body if tok_rows <= 2 * slot_most else sparse_body
    return plan(tokens, grads, route_weights, route_ids, group_picks, frozen_up, factor_a, factor_b)


def solution(mesh):
    return jax.shard_map(
        body,
        mesh=mesh,
        in_specs=(
            P(("rep", "node", "local"), None),
            P(("rep", "node", "local"), None, None),
            P(("rep", "node", "local"), None),
            P(("rep", "node", "local"), None),
            P(("rep", "node", "local"), None),
            P(("node", "local"), None, None),
            P(("node", "local"), None, None),
            P(("node", "local"), None, None),
        ),
        out_specs=(
            P(("rep", "node", "local"), None),
            P(("rep", "node", "local"), None, None),
            P(("rep", "node", "local"), None, None),
        ),
        check_vma=False,
    )
```

```python
import functools
import jax
import jax.numpy as jnp
from jax import lax
from jax.experimental import pallas as pl
from jax.experimental.pallas import tpu as pltpu
from jax.sharding import PartitionSpec as P

GROUPS = 8


adapter_scale_factor = 0.25
weight_gradient_total = 1.0 / 32.0


def slot_ranks(expert_flat, device_count):
    onehot = (expert_flat[:, None] == jnp.arange(device_count, dtype=jnp.int32)[None, :]).astype(
        jnp.int32
    )
    earlier = jnp.cumsum(onehot, axis=0) - onehot
    return jnp.sum(earlier * onehot, axis=1)


def slot_grads(arrived, arrived_grads, frozen, first, second):
    lead = arrived.shape[:-1]
    input_rows = arrived.reshape(-1, arrived.shape[-1])
    gradient_rows = arrived_grads.reshape(-1, arrived_grads.shape[-1])
    rank_space_rows = lax.dot_general(
        gradient_rows, second, (((1,), (1,)), ((), ())), preferred_element_type=jnp.float32
    ).astype(jnp.bfloat16)
    joined_rows = jnp.concatenate([gradient_rows, rank_space_rows], axis=1)
    joined_weight = jnp.concatenate([frozen, first * adapter_scale_factor], axis=1)
    route_gradient = lax.dot_general(
        joined_rows, joined_weight, (((1,), (1,)), ((), ())), preferred_element_type=jnp.float32
    ).astype(jnp.bfloat16)
    projected_rows = jnp.dot(input_rows, first, preferred_element_type=jnp.float32).astype(
        jnp.bfloat16
    )
    return (
        route_gradient.reshape(lead + (frozen.shape[0],)),
        rank_space_rows.reshape(lead + (second.shape[0],)),
        projected_rows.reshape(lead + (second.shape[0],)),
    )


def send_buffers(tokens, scaled, target, device_count, slot_most):
    tok_rows, width = tokens.shape
    pair_count, hidden = scaled.shape
    topk = pair_count // tok_rows
    scaled_pad = jnp.concatenate([scaled, jnp.zeros((1, hidden), jnp.bfloat16)], axis=0)
    tokens_pad = jnp.concatenate([tokens, jnp.zeros((1, width), jnp.bfloat16)], axis=0)
    source = jnp.full((device_count * slot_most,), pair_count, jnp.int32)
    source = source.at[target].set(jnp.arange(pair_count, dtype=jnp.int32))
    owner = jnp.where(source < pair_count, source // topk, tok_rows)
    send_x = tokens_pad[owner].reshape(device_count, slot_most, width)
    send_g = scaled_pad[source].reshape(device_count, slot_most, hidden)
    return (send_x, send_g)


def sparse_body(tokens, grads, route_weights, route_ids, group_picks, frozen_up, factor_a, factor_b):
    tok_rows = tokens.shape[0]
    topk = route_ids.shape[1]
    width = tokens.shape[1]
    hidden = grads.shape[2]
    node_count = lax.axis_size("node")
    local_count = lax.axis_size("local")
    device_count = node_count * local_count
    group_size = device_count // GROUPS
    slot_most = 2 * (5 * tok_rows // 8) // group_size
    pair_count = tok_rows * topk
    frozen = frozen_up[0]
    first = factor_a[0]
    second = factor_b[0]
    experts = jnp.repeat(group_picks, 2, axis=1) * group_size + route_ids
    expert_flat = experts.reshape(-1)
    ranks = slot_ranks(expert_flat, device_count)
    target = expert_flat * slot_most + ranks
    scaled = (
        (grads.astype(jnp.float32) * route_weights[:, :, None])
        .astype(jnp.bfloat16)
        .reshape(pair_count, hidden)
    )
    send_x, send_g = send_buffers(tokens, scaled, target, device_count, slot_most)
    pieces = (
        lax.all_to_all(send_x, ("node", "local"), split_axis=0, concat_axis=0, tiled=True),
        lax.all_to_all(send_g, ("node", "local"), split_axis=0, concat_axis=0, tiled=True),
    )
    route_gradient, rank_space_rows, projected_rows = slot_grads(
        pieces[0], pieces[1], frozen, first, second
    )
    arrived, arrived_grads, route_gradient, rank_space_rows, projected_rows = (
        pieces[0],
        pieces[1],
        route_gradient,
        rank_space_rows,
        projected_rows,
    )
    input_rows = arrived.reshape(-1, width)
    gradient_rows = arrived_grads.reshape(-1, hidden)
    first_factor_gradient = (
        weight_gradient_total
        * adapter_scale_factor
        * lax.dot_general(
            input_rows,
            rank_space_rows.reshape(-1, rank_space_rows.shape[-1]),
            (((0,), (0,)), ((), ())),
            preferred_element_type=jnp.float32,
        )
    )
    second_factor_gradient = (
        weight_gradient_total
        * adapter_scale_factor
        * lax.dot_general(
            projected_rows.reshape(-1, projected_rows.shape[-1]),
            gradient_rows,
            (((0,), (0,)), ((), ())),
            preferred_element_type=jnp.float32,
        )
    )
    returned = lax.all_to_all(
        route_gradient, ("node", "local"), split_axis=0, concat_axis=0, tiled=True
    )
    picked = returned.reshape(-1, width)[target]
    input_grad = jnp.sum(picked.reshape(tok_rows, topk, width).astype(jnp.float32), axis=1).astype(
        jnp.bfloat16
    )
    return (input_grad, first_factor_gradient[None], second_factor_gradient[None])


MESH = pl.DeviceIdType.MESH


def tile_of(width):
    for tile in (512, 256, 128):
        if width % tile == 0:
            return tile
    return width


def visit_order(count):
    table = []
    for z in range(count):
        above, below = list(range(count - 1, z, -1)), list(range(z))
        order = []
        while above or below:
            first, other = (above, below) if len(above) >= len(below) else (below, above)
            order.append(first.pop(0))
            if other:
                order.append(other.pop(0))
        table.append(order + [z])
    return table


def return_kernel(
    z_count, arrived_ref, unpack_ref, frozen_ref, first_ref, second_ref, extra_ref,
    out_ref, fac_ref,
    part, summed, from_y, from_z, lhs, low,
    extra_sem, c_send, c_recv, y_send, y_recv, z_send, z_recv,
):
    f32, bf16 = jnp.float32, jnp.bfloat16
    core = lax.axis_index("node")
    local = lax.axis_index("local")
    z, y = local // 2, lax.rem(local, 2)
    tok_rows = out_ref.shape[0]
    more = fac_ref.shape[0]
    width = out_ref.shape[1]
    tile = tile_of(width)
    nt = (((1,), (1,)), ((), ()))
    table = visit_order(z_count)

    core_peer = {"node": 1 - core}
    y_peer = {"local": z * 2 + 1 - y}

    barrier = pltpu.get_barrier_semaphore()
    pl.semaphore_signal(barrier, inc=1, device_id=core_peer, device_id_type=MESH)
    pl.semaphore_signal(barrier, inc=1, device_id=y_peer, device_id_type=MESH)

    @pl.when(z > 0)
    def _():
        pl.semaphore_signal(barrier, inc=1, device_id={"local": local - 2}, device_id_type=MESH)

    @pl.when(z < z_count - 1)
    def _():
        pl.semaphore_signal(barrier, inc=1, device_id={"local": local + 2}, device_id_type=MESH)

    target = []
    for p in range(z_count):
        zt = jnp.int32(0)
        for i in range(z_count):
            zt = zt + jnp.where(z == i, table[i][p], 0)
        target.append(zt)

    extra_copies = []
    for p in range(z_count):
        copy = pltpu.make_async_copy(
            extra_ref.at[:, target[p]],
            part.at[target[p], :, :, pl.ds(tok_rows, more)],
            extra_sem.at[p],
        )
        copy.start()
        extra_copies.append(copy)

    def compute(p):
        zt = target[p]
        for i in range(4):
            origin = (i // 2) * 2 * z_count + zt * 2 + i % 2
            rows = jnp.dot(unpack_ref[origin], arrived_ref[origin], preferred_element_type=f32)
            lhs[pl.ds(i * tok_rows, tok_rows), :] = rows.astype(bf16)
        low[...] = lax.dot_general(
            lhs[...], second_ref[...], nt, preferred_element_type=f32
        ).astype(bf16)

        @pl.loop(0, width // tile)
        def _(j):
            columns = pl.ds(pl.multiple_of(j * tile, tile), tile)
            value = lax.dot_general(
                lhs[...], frozen_ref[columns, :], nt, preferred_element_type=f32
            ) + lax.dot_general(low[...], first_ref[columns, :], nt, preferred_element_type=f32)
            value = value.astype(bf16)
            for i in range(4):
                part[zt, i // 2, i % 2, pl.ds(0, tok_rows), columns] = value[
                    i * tok_rows : (i + 1) * tok_rows
                ]

        extra_copies[p].wait()

    def c_copy(p):
        return pltpu.make_async_remote_copy(
            part.at[target[p], 1 - core], summed.at[target[p]], c_send.at[p], c_recv.at[p],
            device_id=core_peer, device_id_type=MESH,
        )

    def y_copy(p):
        return pltpu.make_async_remote_copy(
            summed.at[target[p], 1 - y], from_y.at[target[p]], y_send.at[p], y_recv.at[p],
            device_id=y_peer, device_id_type=MESH,
        )

    def over_rows(count, step):
        @pl.loop(0, count // 16)
        def _(i):
            step(pl.ds(pl.multiple_of(i * 16, 16), 16))

    def add_core(p):
        zt = target[p]
        c_copy(p).wait_recv()
        for half in (1 - y, y):

            def step(rows):
                summed[zt, half, rows, :] = (
                    summed[zt, half, rows, :].astype(f32) + part[zt, core, half, rows, :].astype(f32)
                ).astype(bf16)

            over_rows(tok_rows + more, step)
            if half is not y:
                y_copy(p).start()

    compute(0)
    neighbours = 2 + jnp.where(z > 0, 1, 0) + jnp.where(z < z_count - 1, 1, 0)
    pl.semaphore_wait(barrier, neighbours)
    c_copy(0).start()
    for p in range(1, z_count):
        compute(p)
        c_copy(p).start()
        add_core(p - 1)
    add_core(z_count - 1)

    def z_copy(p, slot, peer):
        return pltpu.make_async_remote_copy(
            summed.at[target[p], y], from_z.at[slot], z_send.at[p], z_recv.at[slot],
            device_id={"local": peer}, device_id_type=MESH,
        )

    def slot_wait(slot):
        z_copy(0, slot, local).wait_recv()

    for p in range(z_count - 1):
        zt = target[p]
        up = zt > z
        y_copy(p).wait_recv()
        passing = jnp.logical_or(jnp.logical_and(up, z > 0), jnp.logical_and(zt < z, z < z_count - 1))

        @pl.when(passing)
        def _():
            slot_wait(zt)

            def step(rows):
                summed[zt, y, rows, :] = (
                    summed[zt, y, rows, :].astype(f32)
                    + from_y[zt, rows, :].astype(f32)
                    + from_z[zt, rows, :].astype(f32)
                ).astype(bf16)

            over_rows(tok_rows + more, step)

        @pl.when(jnp.logical_not(passing))
        def _():
            def step(rows):
                summed[zt, y, rows, :] = (
                    summed[zt, y, rows, :].astype(f32) + from_y[zt, rows, :].astype(f32)
                ).astype(bf16)

            over_rows(tok_rows + more, step)

        slot = jnp.where(zt == z - 1, z_count, zt)
        z_copy(p, slot, jnp.where(up, local + 2, local - 2)).start()

    p = z_count - 1
    y_copy(p).wait_recv()

    def finish(with_below, with_above):
        def total(rows):
            value = summed[z, y, rows, :].astype(f32) + from_y[z, rows, :].astype(f32)
            if with_below:
                value = value + from_z[z, rows, :].astype(f32)
            if with_above:
                value = value + from_z[z_count, rows, :].astype(f32)
            return value

        if with_below:
            slot_wait(z)
        if with_above:
            slot_wait(z_count)

        def step(rows):
            out_ref[rows, :] = total(rows).astype(bf16)

        over_rows(tok_rows, step)
        for start in range(0, more, 16):
            fac_ref[pl.ds(start, 16), :] = total(pl.ds(tok_rows + start, 16))

    @pl.when(z == 0)
    def _():
        finish(False, True)

    @pl.when(z == z_count - 1)
    def _():
        finish(True, False)

    @pl.when(jnp.logical_and(z > 0, z < z_count - 1))
    def _():
        finish(True, True)

    for p in range(z_count):
        c_copy(p).wait_send()
        y_copy(p).wait_send()
    for p in range(z_count - 1):
        z_copy(p, 0, local).wait_send()


def return_sums(arrived, unpack, frozen, first, second, extra, tok_rows):
    bf16 = jnp.bfloat16
    z_count, more, width = extra.shape[1], extra.shape[3], extra.shape[4]
    rows = tok_rows + more
    dma = pltpu.SemaphoreType.DMA
    vmem = pl.BlockSpec(memory_space=pltpu.VMEM)
    routes = 4 * z_count * tok_rows
    return pl.pallas_call(
        functools.partial(return_kernel, z_count),
        out_shape=(
            jax.ShapeDtypeStruct((tok_rows, width), bf16),
            jax.ShapeDtypeStruct((more, width), jnp.float32),
        ),
        in_specs=[vmem] * 5 + [pl.BlockSpec(memory_space=pl.ANY)],
        out_specs=(vmem, vmem),
        scratch_shapes=[
            pltpu.VMEM((z_count, 2, 2, rows, width), bf16),
            pltpu.VMEM((z_count, 2, rows, width), bf16),
            pltpu.VMEM((z_count, rows, width), bf16),
            pltpu.VMEM((z_count + 1, rows, width), bf16),
            pltpu.VMEM((4 * tok_rows, frozen.shape[1]), bf16),
            pltpu.VMEM((4 * tok_rows, second.shape[0]), bf16),
            dma((z_count,)), dma((z_count,)), dma((z_count,)), dma((z_count,)),
            dma((z_count,)), dma((z_count,)), dma((z_count + 1,)),
        ],
        compiler_params=pltpu.CompilerParams(
            collective_id=0, has_side_effects=True, vmem_limit_bytes=60 * 2**20
        ),
        cost_estimate=pl.CostEstimate(
            flops=2 * routes * width * frozen.shape[1], bytes_accessed=20 * 2**20, transcendentals=0
        ),
    )(arrived, unpack, frozen, first, second, extra)


def scale_routes(grads, route_weights):
    pair_count = grads.shape[0] * grads.shape[1]
    return (
        (grads.astype(jnp.float32) * route_weights[:, :, None])
        .astype(jnp.bfloat16)
        .reshape(pair_count, grads.shape[2])
    )


def dense_body(tokens, grads, route_weights, route_ids, group_picks, frozen_up, factor_a, factor_b):
    tok_rows, width = tokens.shape
    topk = route_ids.shape[1]
    hidden = grads.shape[2]
    rank = factor_b.shape[1]
    axes = ("node", "local")
    device_count = lax.axis_size("node") * lax.axis_size("local")
    me = lax.axis_index("node") * lax.axis_size("local") + lax.axis_index("local")
    group_size = device_count // GROUPS
    slot_most = 2 * (5 * tok_rows // 8) // group_size
    f32, bf16 = jnp.float32, jnp.bfloat16
    experts = jnp.repeat(group_picks, 2, axis=1) * group_size + route_ids
    expert_flat = experts.reshape(-1)
    first_t = factor_a[0].T
    second = factor_b[0]
    table = jnp.zeros((rank, tok_rows), bf16).at[:topk].set(experts.T.astype(bf16))
    shared = lax.all_gather(
        jnp.concatenate([first_t, second, table], axis=1), axes, axis=0, tiled=True
    )
    all_first = shared[:, :width]
    all_second = shared[:, width : width + hidden]
    tables = shared[:, width + hidden :].reshape(device_count, rank, tok_rows)[:, :topk]

    ids = jnp.arange(device_count, dtype=jnp.int32)
    member = (experts[:, :, None] == ids[None, None, :]).any(axis=1)
    order = jnp.cumsum(member.astype(jnp.int32), axis=0) - 1
    ranks = jnp.sum(jnp.where(experts[:, :, None] == ids, order[:, None, :], 0), axis=2)
    target = experts * slot_most + ranks
    scaled = scale_routes(grads, route_weights)
    slots = jnp.arange(device_count * slot_most, dtype=jnp.int32)
    pack = (target.reshape(1, -1) == slots[:, None]).astype(bf16)
    send_g = jnp.dot(pack, scaled, preferred_element_type=f32).astype(bf16)
    arrived = lax.all_to_all(
        send_g.reshape(device_count, slot_most, hidden), axes, split_axis=0, concat_axis=0, tiled=True
    )

    owner_mask = expert_flat[:, None] == jnp.repeat(ids, rank)[None, :]
    middle = lax.dot_general(scaled, all_second, (((1,), (1,)), ((), ())), preferred_element_type=f32)
    middle = jnp.where(owner_mask, middle, 0.0).reshape(tok_rows, topk, -1).sum(axis=1).astype(bf16)
    projected = lax.dot_general(
        tokens, all_first, (((1,), (1,)), ((), ())), preferred_element_type=f32
    ).astype(bf16)
    projected = jnp.where(
        owner_mask.reshape(tok_rows, topk, -1), projected[:, None, :], jnp.zeros((), bf16)
    ).reshape(tok_rows * topk, -1)
    share_a = lax.dot_general(middle, tokens, (((0,), (0,)), ((), ())), preferred_element_type=f32)
    share_b = lax.dot_general(projected, scaled, (((0,), (0,)), ((), ())), preferred_element_type=f32)
    half = rank // 2
    share_b = share_b.astype(bf16).reshape(device_count, 2, half, hidden)
    share_b = jnp.concatenate([share_b[:, 0], share_b[:, 1]], axis=2)
    share_b = jnp.pad(share_b, ((0, 0), (0, 0), (0, width - 2 * hidden)))
    extra = jnp.concatenate(
        [share_a.astype(bf16).reshape(device_count, rank, width), share_b], axis=1
    ).reshape(2, device_count // 4, 2, rank + half, width)

    mine = (tables == me.astype(bf16)).any(axis=1)
    place = jnp.cumsum(mine.astype(jnp.int32), axis=1) - 1
    unpack = (
        mine[:, :, None] & (place[:, :, None] == jnp.arange(slot_most, dtype=jnp.int32))
    ).astype(bf16)
    input_grad, factor_sums = return_sums(
        arrived, unpack, frozen_up[0], factor_a[0] * adapter_scale_factor, second, extra, tok_rows
    )
    factor_sums = factor_sums * (weight_gradient_total * adapter_scale_factor)
    grad_a = factor_sums[:rank].T[None]
    last = factor_sums[rank:]
    grad_b = jnp.concatenate([last[:, :hidden], last[:, hidden : 2 * hidden]], axis=0)[None]
    return (input_grad, grad_a, grad_b)


def body(tokens, grads, route_weights, route_ids, group_picks, frozen_up, factor_a, factor_b):
    tok_rows = tokens.shape[0]
    group_size = lax.axis_size("node") * lax.axis_size("local") // GROUPS
    slot_most = 2 * (5 * tok_rows // 8) // group_size
    plan = dense_body if tok_rows <= 2 * slot_most else sparse_body
    return plan(tokens, grads, route_weights, route_ids, group_picks, frozen_up, factor_a, factor_b)


def solution(mesh):
    return jax.shard_map(
        body,
        mesh=mesh,
        in_specs=(
            P(("rep", "node", "local"), None),
            P(("rep", "node", "local"), None, None),
            P(("rep", "node", "local"), None),
            P(("rep", "node", "local"), None),
            P(("rep", "node", "local"), None),
            P(("node", "local"), None, None),
            P(("node", "local"), None, None),
            P(("node", "local"), None, None),
        ),
        out_specs=(
            P(("rep", "node", "local"), None),
            P(("rep", "node", "local"), None, None),
            P(("rep", "node", "local"), None, None),
        ),
        check_vma=False,
    )
```

```python
import functools
import jax
import jax.numpy as jnp
from jax import lax
from jax.experimental import pallas as pl
from jax.experimental.pallas import tpu as pltpu
from jax.sharding import PartitionSpec as P

GROUPS = 8


adapter_scale_factor = 0.25
weight_gradient_total = 1.0 / 32.0


def slot_ranks(expert_flat, device_count):
    onehot = (expert_flat[:, None] == jnp.arange(device_count, dtype=jnp.int32)[None, :]).astype(
        jnp.int32
    )
    earlier = jnp.cumsum(onehot, axis=0) - onehot
    return jnp.sum(earlier * onehot, axis=1)


def slot_grads(arrived, arrived_grads, frozen, first, second):
    lead = arrived.shape[:-1]
    input_rows = arrived.reshape(-1, arrived.shape[-1])
    gradient_rows = arrived_grads.reshape(-1, arrived_grads.shape[-1])
    rank_space_rows = lax.dot_general(
        gradient_rows, second, (((1,), (1,)), ((), ())), preferred_element_type=jnp.float32
    ).astype(jnp.bfloat16)
    joined_rows = jnp.concatenate([gradient_rows, rank_space_rows], axis=1)
    joined_weight = jnp.concatenate([frozen, first * adapter_scale_factor], axis=1)
    route_gradient = lax.dot_general(
        joined_rows, joined_weight, (((1,), (1,)), ((), ())), preferred_element_type=jnp.float32
    ).astype(jnp.bfloat16)
    projected_rows = jnp.dot(input_rows, first, preferred_element_type=jnp.float32).astype(
        jnp.bfloat16
    )
    return (
        route_gradient.reshape(lead + (frozen.shape[0],)),
        rank_space_rows.reshape(lead + (second.shape[0],)),
        projected_rows.reshape(lead + (second.shape[0],)),
    )


def send_buffers(tokens, scaled, target, device_count, slot_most):
    tok_rows, width = tokens.shape
    pair_count, hidden = scaled.shape
    topk = pair_count // tok_rows
    scaled_pad = jnp.concatenate([scaled, jnp.zeros((1, hidden), jnp.bfloat16)], axis=0)
    tokens_pad = jnp.concatenate([tokens, jnp.zeros((1, width), jnp.bfloat16)], axis=0)
    source = jnp.full((device_count * slot_most,), pair_count, jnp.int32)
    source = source.at[target].set(jnp.arange(pair_count, dtype=jnp.int32))
    owner = jnp.where(source < pair_count, source // topk, tok_rows)
    send_x = tokens_pad[owner].reshape(device_count, slot_most, width)
    send_g = scaled_pad[source].reshape(device_count, slot_most, hidden)
    return (send_x, send_g)


def sparse_body(tokens, grads, route_weights, route_ids, group_picks, frozen_up, factor_a, factor_b):
    tok_rows = tokens.shape[0]
    topk = route_ids.shape[1]
    width = tokens.shape[1]
    hidden = grads.shape[2]
    node_count = lax.axis_size("node")
    local_count = lax.axis_size("local")
    device_count = node_count * local_count
    group_size = device_count // GROUPS
    slot_most = 2 * (5 * tok_rows // 8) // group_size
    pair_count = tok_rows * topk
    frozen = frozen_up[0]
    first = factor_a[0]
    second = factor_b[0]
    experts = jnp.repeat(group_picks, 2, axis=1) * group_size + route_ids
    expert_flat = experts.reshape(-1)
    ranks = slot_ranks(expert_flat, device_count)
    target = expert_flat * slot_most + ranks
    scaled = (
        (grads.astype(jnp.float32) * route_weights[:, :, None])
        .astype(jnp.bfloat16)
        .reshape(pair_count, hidden)
    )
    send_x, send_g = send_buffers(tokens, scaled, target, device_count, slot_most)
    pieces = (
        lax.all_to_all(send_x, ("node", "local"), split_axis=0, concat_axis=0, tiled=True),
        lax.all_to_all(send_g, ("node", "local"), split_axis=0, concat_axis=0, tiled=True),
    )
    route_gradient, rank_space_rows, projected_rows = slot_grads(
        pieces[0], pieces[1], frozen, first, second
    )
    arrived, arrived_grads, route_gradient, rank_space_rows, projected_rows = (
        pieces[0],
        pieces[1],
        route_gradient,
        rank_space_rows,
        projected_rows,
    )
    input_rows = arrived.reshape(-1, width)
    gradient_rows = arrived_grads.reshape(-1, hidden)
    first_factor_gradient = (
        weight_gradient_total
        * adapter_scale_factor
        * lax.dot_general(
            input_rows,
            rank_space_rows.reshape(-1, rank_space_rows.shape[-1]),
            (((0,), (0,)), ((), ())),
            preferred_element_type=jnp.float32,
        )
    )
    second_factor_gradient = (
        weight_gradient_total
        * adapter_scale_factor
        * lax.dot_general(
            projected_rows.reshape(-1, projected_rows.shape[-1]),
            gradient_rows,
            (((0,), (0,)), ((), ())),
            preferred_element_type=jnp.float32,
        )
    )
    returned = lax.all_to_all(
        route_gradient, ("node", "local"), split_axis=0, concat_axis=0, tiled=True
    )
    picked = returned.reshape(-1, width)[target]
    input_grad = jnp.sum(picked.reshape(tok_rows, topk, width).astype(jnp.float32), axis=1).astype(
        jnp.bfloat16
    )
    return (input_grad, first_factor_gradient[None], second_factor_gradient[None])


MESH = pl.DeviceIdType.MESH


def tile_of(width):
    for tile in (512, 256, 128):
        if width % tile == 0:
            return tile
    return width


def visit_order(count):
    table = []
    for z in range(count):
        above, below = list(range(count - 1, z, -1)), list(range(z))
        order = []
        while above or below:
            first, other = (above, below) if len(above) >= len(below) else (below, above)
            order.append(first.pop(0))
            if other:
                order.append(other.pop(0))
        table.append(order + [z])
    return table


def return_kernel(
    z_count, arrived_ref, unpack_ref, frozen_ref, first_ref, second_ref, extra_ref,
    out_ref, fac_ref,
    part, summed, from_y, from_z, lhs, low,
    extra_sem, c_send, c_recv, y_send, y_recv, z_send, z_recv,
):
    f32, bf16 = jnp.float32, jnp.bfloat16
    core = lax.axis_index("node")
    local = lax.axis_index("local")
    z, y = local // 2, lax.rem(local, 2)
    tok_rows = out_ref.shape[0]
    more = fac_ref.shape[0]
    width = out_ref.shape[1]
    tile = tile_of(width)
    nt = (((1,), (1,)), ((), ()))
    table = visit_order(z_count)

    core_peer = {"node": 1 - core}
    y_peer = {"local": z * 2 + 1 - y}

    barrier = pltpu.get_barrier_semaphore()
    pl.semaphore_signal(barrier, inc=1, device_id=core_peer, device_id_type=MESH)
    pl.semaphore_signal(barrier, inc=1, device_id=y_peer, device_id_type=MESH)

    @pl.when(z > 0)
    def _():
        pl.semaphore_signal(barrier, inc=1, device_id={"local": local - 2}, device_id_type=MESH)

    @pl.when(z < z_count - 1)
    def _():
        pl.semaphore_signal(barrier, inc=1, device_id={"local": local + 2}, device_id_type=MESH)

    target = []
    for p in range(z_count):
        zt = jnp.int32(0)
        for i in range(z_count):
            zt = zt + jnp.where(z == i, table[i][p], 0)
        target.append(zt)

    extra_copies = []
    for p in range(z_count):
        copy = pltpu.make_async_copy(
            extra_ref.at[:, target[p]],
            part.at[target[p], :, :, pl.ds(tok_rows, more)],
            extra_sem.at[p],
        )
        copy.start()
        extra_copies.append(copy)

    def compute(p):
        zt = target[p]
        for i in range(4):
            origin = (i // 2) * 2 * z_count + zt * 2 + i % 2
            rows = jnp.dot(unpack_ref[origin], arrived_ref[origin], preferred_element_type=f32)
            lhs[pl.ds(i * tok_rows, tok_rows), :] = rows.astype(bf16)
        low[...] = lax.dot_general(
            lhs[...], second_ref[...], nt, preferred_element_type=f32
        ).astype(bf16)

        @pl.loop(0, width // tile)
        def _(j):
            columns = pl.ds(pl.multiple_of(j * tile, tile), tile)
            value = lax.dot_general(
                lhs[...], frozen_ref[columns, :], nt, preferred_element_type=f32
            ) + lax.dot_general(low[...], first_ref[columns, :], nt, preferred_element_type=f32)
            value = value.astype(bf16)
            for i in range(4):
                part[zt, i // 2, i % 2, pl.ds(0, tok_rows), columns] = value[
                    i * tok_rows : (i + 1) * tok_rows
                ]

        extra_copies[p].wait()

    def c_copy(p):
        return pltpu.make_async_remote_copy(
            part.at[target[p], 1 - core], summed.at[target[p]], c_send.at[p], c_recv.at[p],
            device_id=core_peer, device_id_type=MESH,
        )

    def y_copy(p):
        return pltpu.make_async_remote_copy(
            summed.at[target[p], 1 - y], from_y.at[target[p]], y_send.at[p], y_recv.at[p],
            device_id=y_peer, device_id_type=MESH,
        )

    def over_rows(count, step):
        @pl.loop(0, count // 16)
        def _(i):
            step(pl.ds(pl.multiple_of(i * 16, 16), 16))

    def add_core(p):
        zt = target[p]
        c_copy(p).wait_recv()
        for half in (1 - y, y):

            def step(rows):
                summed[zt, half, rows, :] = (
                    summed[zt, half, rows, :].astype(f32) + part[zt, core, half, rows, :].astype(f32)
                ).astype(bf16)

            over_rows(tok_rows + more, step)
            if half is not y:
                y_copy(p).start()

    compute(0)
    neighbours = 2 + jnp.where(z > 0, 1, 0) + jnp.where(z < z_count - 1, 1, 0)
    pl.semaphore_wait(barrier, neighbours)
    c_copy(0).start()
    for p in range(1, z_count):
        compute(p)
        c_copy(p).start()
        add_core(p - 1)
    add_core(z_count - 1)

    def z_copy(p, slot, peer):
        return pltpu.make_async_remote_copy(
            summed.at[target[p], y], from_z.at[slot], z_send.at[p], z_recv.at[slot],
            device_id={"local": peer}, device_id_type=MESH,
        )

    def slot_wait(slot):
        z_copy(0, slot, local).wait_recv()

    for p in range(z_count - 1):
        zt = target[p]
        up = zt > z
        y_copy(p).wait_recv()
        passing = jnp.logical_or(jnp.logical_and(up, z > 0), jnp.logical_and(zt < z, z < z_count - 1))

        @pl.when(passing)
        def _():
            slot_wait(zt)

            def step(rows):
                summed[zt, y, rows, :] = (
                    summed[zt, y, rows, :].astype(f32)
                    + from_y[zt, rows, :].astype(f32)
                    + from_z[zt, rows, :].astype(f32)
                ).astype(bf16)

            over_rows(tok_rows + more, step)

        @pl.when(jnp.logical_not(passing))
        def _():
            def step(rows):
                summed[zt, y, rows, :] = (
                    summed[zt, y, rows, :].astype(f32) + from_y[zt, rows, :].astype(f32)
                ).astype(bf16)

            over_rows(tok_rows + more, step)

        slot = jnp.where(zt == z - 1, z_count, zt)
        z_copy(p, slot, jnp.where(up, local + 2, local - 2)).start()

    p = z_count - 1
    y_copy(p).wait_recv()

    def finish(with_below, with_above):
        def total(rows):
            value = summed[z, y, rows, :].astype(f32) + from_y[z, rows, :].astype(f32)
            if with_below:
                value = value + from_z[z, rows, :].astype(f32)
            if with_above:
                value = value + from_z[z_count, rows, :].astype(f32)
            return value

        if with_below:
            slot_wait(z)
        if with_above:
            slot_wait(z_count)

        def step(rows):
            out_ref[rows, :] = total(rows).astype(bf16)

        over_rows(tok_rows, step)
        for start in range(0, more, 16):
            fac_ref[pl.ds(start, 16), :] = total(pl.ds(tok_rows + start, 16))

    @pl.when(z == 0)
    def _():
        finish(False, True)

    @pl.when(z == z_count - 1)
    def _():
        finish(True, False)

    @pl.when(jnp.logical_and(z > 0, z < z_count - 1))
    def _():
        finish(True, True)

    for p in range(z_count):
        c_copy(p).wait_send()
        y_copy(p).wait_send()
    for p in range(z_count - 1):
        z_copy(p, 0, local).wait_send()


def return_sums(arrived, unpack, frozen, first, second, extra, tok_rows):
    bf16 = jnp.bfloat16
    z_count, more, width = extra.shape[1], extra.shape[3], extra.shape[4]
    rows = tok_rows + more
    dma = pltpu.SemaphoreType.DMA
    vmem = pl.BlockSpec(memory_space=pltpu.VMEM)
    routes = 4 * z_count * tok_rows
    return pl.pallas_call(
        functools.partial(return_kernel, z_count),
        out_shape=(
            jax.ShapeDtypeStruct((tok_rows, width), bf16),
            jax.ShapeDtypeStruct((more, width), jnp.float32),
        ),
        in_specs=[vmem] * 5 + [pl.BlockSpec(memory_space=pl.ANY)],
        out_specs=(vmem, vmem),
        scratch_shapes=[
            pltpu.VMEM((z_count, 2, 2, rows, width), bf16),
            pltpu.VMEM((z_count, 2, rows, width), bf16),
            pltpu.VMEM((z_count, rows, width), bf16),
            pltpu.VMEM((z_count + 1, rows, width), bf16),
            pltpu.VMEM((4 * tok_rows, frozen.shape[1]), bf16),
            pltpu.VMEM((4 * tok_rows, second.shape[0]), bf16),
            dma((z_count,)), dma((z_count,)), dma((z_count,)), dma((z_count,)),
            dma((z_count,)), dma((z_count,)), dma((z_count + 1,)),
        ],
        compiler_params=pltpu.CompilerParams(
            collective_id=0, has_side_effects=True, vmem_limit_bytes=60 * 2**20
        ),
        cost_estimate=pl.CostEstimate(
            flops=2 * routes * width * frozen.shape[1], bytes_accessed=20 * 2**20, transcendentals=0
        ),
    )(arrived, unpack, frozen, first, second, extra)


def gather_kernel(z_count, own_ref, all_ref, own_sem, recv, up_send, down_send, y_send, c_send):
    core = lax.axis_index("node")
    local = lax.axis_index("local")
    z, y = local // 2, lax.rem(local, 2)
    core_peer = {"node": 1 - core}
    y_peer = {"local": z * 2 + 1 - y}
    above, below = {"local": local + 2}, {"local": local - 2}
    has_above, has_below = z < z_count - 1, z > 0

    barrier = pltpu.get_barrier_semaphore()
    pl.semaphore_signal(barrier, inc=1, device_id=core_peer, device_id_type=MESH)
    pl.semaphore_signal(barrier, inc=1, device_id=y_peer, device_id_type=MESH)

    @pl.when(has_below)
    def _():
        pl.semaphore_signal(barrier, inc=1, device_id=below, device_id_type=MESH)

    @pl.when(has_above)
    def _():
        pl.semaphore_signal(barrier, inc=1, device_id=above, device_id_type=MESH)

    place = pltpu.make_async_copy(own_ref, all_ref.at[core, z, y], own_sem)
    place.start()
    place.wait()
    neighbours = 2 + jnp.where(has_below, 1, 0) + jnp.where(has_above, 1, 0)
    pl.semaphore_wait(barrier, neighbours)

    def copy(zs, ys, send_sem, peer):
        return pltpu.make_async_remote_copy(
            all_ref.at[core, zs, ys], all_ref.at[core, zs, ys], send_sem, recv.at[core, zs, ys],
            device_id=peer, device_id_type=MESH,
        )

    def arrival(cs, zs, ys):
        pltpu.make_async_remote_copy(
            all_ref.at[cs, zs, ys], all_ref.at[cs, zs, ys], own_sem, recv.at[cs, zs, ys],
            device_id=core_peer, device_id_type=MESH,
        ).wait_recv()

    def spread(zs):
        copy(zs, y, y_send.at[zs], y_peer).start()
        copy(zs, y, c_send.at[zs, y], core_peer).start()

    @pl.when(has_above)
    def _():
        copy(z, y, up_send.at[z], above).start()

    @pl.when(has_below)
    def _():
        copy(z, y, down_send.at[z], below).start()

    spread(z)
    for distance in range(1, z_count):

        @pl.when(z - distance >= 0)
        def _():
            zs = z - distance
            arrival(core, zs, y)

            @pl.when(has_above)
            def _():
                copy(zs, y, up_send.at[zs], above).start()

            spread(zs)

        @pl.when(z + distance < z_count)
        def _():
            zs = z + distance
            arrival(core, zs, y)

            @pl.when(has_below)
            def _():
                copy(zs, y, down_send.at[zs], below).start()

            spread(zs)

    def from_y(zs):
        arrival(core, zs, 1 - y)
        copy(zs, 1 - y, c_send.at[zs, 1 - y], core_peer).start()

    from_y(z)
    for distance in range(1, z_count):

        @pl.when(z - distance >= 0)
        def _():
            from_y(z - distance)

        @pl.when(z + distance < z_count)
        def _():
            from_y(z + distance)

    for zs in range(z_count):
        for ys in range(2):
            arrival(1 - core, zs, ys)
            copy(zs, ys, c_send.at[zs, ys], core_peer).wait_send()
        copy(zs, y, y_send.at[zs], y_peer).wait_send()

        @pl.when(jnp.logical_and(has_above, zs <= z))
        def _():
            copy(zs, y, up_send.at[zs], core_peer).wait_send()

        @pl.when(jnp.logical_and(has_below, zs >= z))
        def _():
            copy(zs, y, down_send.at[zs], core_peer).wait_send()


def gather_shards(own, device_count):
    z_count = device_count // 4
    dma = pltpu.SemaphoreType.DMA
    vmem = pl.BlockSpec(memory_space=pltpu.VMEM)
    gathered = pl.pallas_call(
        functools.partial(gather_kernel, z_count),
        out_shape=jax.ShapeDtypeStruct((2, z_count, 2) + own.shape, own.dtype),
        in_specs=[vmem],
        out_specs=vmem,
        scratch_shapes=[
            dma, dma((2, z_count, 2)), dma((z_count,)), dma((z_count,)),
            dma((z_count,)), dma((z_count, 2)),
        ],
        compiler_params=pltpu.CompilerParams(
            collective_id=1, has_side_effects=True, vmem_limit_bytes=24 * 2**20
        ),
        cost_estimate=pl.CostEstimate(flops=0, bytes_accessed=100 * 2**20, transcendentals=0),
    )(own)
    return gathered.reshape((device_count * own.shape[0],) + own.shape[1:])


def scale_routes(grads, route_weights):
    pair_count = grads.shape[0] * grads.shape[1]
    return (
        (grads.astype(jnp.float32) * route_weights[:, :, None])
        .astype(jnp.bfloat16)
        .reshape(pair_count, grads.shape[2])
    )


def dense_body(tokens, grads, route_weights, route_ids, group_picks, frozen_up, factor_a, factor_b):
    tok_rows, width = tokens.shape
    topk = route_ids.shape[1]
    hidden = grads.shape[2]
    rank = factor_b.shape[1]
    axes = ("node", "local")
    device_count = lax.axis_size("node") * lax.axis_size("local")
    me = lax.axis_index("node") * lax.axis_size("local") + lax.axis_index("local")
    group_size = device_count // GROUPS
    slot_most = 2 * (5 * tok_rows // 8) // group_size
    f32, bf16 = jnp.float32, jnp.bfloat16
    experts = jnp.repeat(group_picks, 2, axis=1) * group_size + route_ids
    expert_flat = experts.reshape(-1)
    first_t = factor_a[0].T
    second = factor_b[0]
    table = jnp.zeros((rank, tok_rows), bf16).at[:topk].set(experts.T.astype(bf16))
    ids = jnp.arange(device_count, dtype=jnp.int32)
    member = (experts[:, :, None] == ids[None, None, :]).any(axis=1)
    order = jnp.cumsum(member.astype(jnp.int32), axis=0) - 1
    ranks = jnp.sum(jnp.where(experts[:, :, None] == ids, order[:, None, :], 0), axis=2)
    target = experts * slot_most + ranks
    scaled = scale_routes(grads, route_weights)
    slots = jnp.arange(device_count * slot_most, dtype=jnp.int32)
    pack = (target.reshape(1, -1) == slots[:, None]).astype(bf16)
    send_g = jnp.dot(pack, scaled, preferred_element_type=f32).astype(bf16)
    own = jnp.concatenate([first_t, second, table], axis=1)
    own, send_g = lax.optimization_barrier((own, send_g))
    arrived = lax.all_to_all(
        send_g.reshape(device_count, slot_most, hidden), axes, split_axis=0, concat_axis=0, tiled=True
    )

    shared = gather_shards(own, device_count)
    all_first = shared[:, :width]
    all_second = shared[:, width : width + hidden]
    tables = shared[:, width + hidden :].reshape(device_count, rank, tok_rows)[:, :topk]

    owner_mask = expert_flat[:, None] == jnp.repeat(ids, rank)[None, :]
    middle = lax.dot_general(scaled, all_second, (((1,), (1,)), ((), ())), preferred_element_type=f32)
    middle = jnp.where(owner_mask, middle, 0.0).reshape(tok_rows, topk, -1).sum(axis=1).astype(bf16)
    projected = lax.dot_general(
        tokens, all_first, (((1,), (1,)), ((), ())), preferred_element_type=f32
    ).astype(bf16)
    projected = jnp.where(
        owner_mask.reshape(tok_rows, topk, -1), projected[:, None, :], jnp.zeros((), bf16)
    ).reshape(tok_rows * topk, -1)
    share_a = lax.dot_general(middle, tokens, (((0,), (0,)), ((), ())), preferred_element_type=f32)
    share_b = lax.dot_general(projected, scaled, (((0,), (0,)), ((), ())), preferred_element_type=f32)
    half = rank // 2
    share_b = share_b.astype(bf16).reshape(device_count, 2, half, hidden)
    share_b = jnp.concatenate([share_b[:, 0], share_b[:, 1]], axis=2)
    share_b = jnp.pad(share_b, ((0, 0), (0, 0), (0, width - 2 * hidden)))
    extra = jnp.concatenate(
        [share_a.astype(bf16).reshape(device_count, rank, width), share_b], axis=1
    ).reshape(2, device_count // 4, 2, rank + half, width)

    mine = (tables == me.astype(bf16)).any(axis=1)
    place = jnp.cumsum(mine.astype(jnp.int32), axis=1) - 1
    unpack = (
        mine[:, :, None] & (place[:, :, None] == jnp.arange(slot_most, dtype=jnp.int32))
    ).astype(bf16)
    input_grad, factor_sums = return_sums(
        arrived, unpack, frozen_up[0], factor_a[0] * adapter_scale_factor, second, extra, tok_rows
    )
    factor_sums = factor_sums * (weight_gradient_total * adapter_scale_factor)
    grad_a = factor_sums[:rank].T[None]
    last = factor_sums[rank:]
    grad_b = jnp.concatenate([last[:, :hidden], last[:, hidden : 2 * hidden]], axis=0)[None]
    return (input_grad, grad_a, grad_b)


def body(tokens, grads, route_weights, route_ids, group_picks, frozen_up, factor_a, factor_b):
    tok_rows = tokens.shape[0]
    group_size = lax.axis_size("node") * lax.axis_size("local") // GROUPS
    slot_most = 2 * (5 * tok_rows // 8) // group_size
    plan = dense_body if tok_rows <= 2 * slot_most else sparse_body
    return plan(tokens, grads, route_weights, route_ids, group_picks, frozen_up, factor_a, factor_b)


def solution(mesh):
    return jax.shard_map(
        body,
        mesh=mesh,
        in_specs=(
            P(("rep", "node", "local"), None),
            P(("rep", "node", "local"), None, None),
            P(("rep", "node", "local"), None),
            P(("rep", "node", "local"), None),
            P(("rep", "node", "local"), None),
            P(("node", "local"), None, None),
            P(("node", "local"), None, None),
            P(("node", "local"), None, None),
        ),
        out_specs=(
            P(("rep", "node", "local"), None),
            P(("rep", "node", "local"), None, None),
            P(("rep", "node", "local"), None, None),
        ),
        check_vma=False,
    )
```

```python
import functools
import jax
import jax.numpy as jnp
from jax import lax
from jax.experimental import pallas as pl
from jax.experimental.pallas import tpu as pltpu
from jax.sharding import PartitionSpec as P

GROUPS = 8


adapter_scale_factor = 0.25
weight_gradient_total = 1.0 / 32.0


def slot_ranks(expert_flat, device_count):
    onehot = (expert_flat[:, None] == jnp.arange(device_count, dtype=jnp.int32)[None, :]).astype(
        jnp.int32
    )
    earlier = jnp.cumsum(onehot, axis=0) - onehot
    return jnp.sum(earlier * onehot, axis=1)


def slot_grads(arrived, arrived_grads, frozen, first, second):
    lead = arrived.shape[:-1]
    input_rows = arrived.reshape(-1, arrived.shape[-1])
    gradient_rows = arrived_grads.reshape(-1, arrived_grads.shape[-1])
    rank_space_rows = lax.dot_general(
        gradient_rows, second, (((1,), (1,)), ((), ())), preferred_element_type=jnp.float32
    ).astype(jnp.bfloat16)
    joined_rows = jnp.concatenate([gradient_rows, rank_space_rows], axis=1)
    joined_weight = jnp.concatenate([frozen, first * adapter_scale_factor], axis=1)
    route_gradient = lax.dot_general(
        joined_rows, joined_weight, (((1,), (1,)), ((), ())), preferred_element_type=jnp.float32
    ).astype(jnp.bfloat16)
    projected_rows = jnp.dot(input_rows, first, preferred_element_type=jnp.float32).astype(
        jnp.bfloat16
    )
    return (
        route_gradient.reshape(lead + (frozen.shape[0],)),
        rank_space_rows.reshape(lead + (second.shape[0],)),
        projected_rows.reshape(lead + (second.shape[0],)),
    )


def send_buffers(tokens, scaled, target, device_count, slot_most):
    tok_rows, width = tokens.shape
    pair_count, hidden = scaled.shape
    topk = pair_count // tok_rows
    scaled_pad = jnp.concatenate([scaled, jnp.zeros((1, hidden), jnp.bfloat16)], axis=0)
    tokens_pad = jnp.concatenate([tokens, jnp.zeros((1, width), jnp.bfloat16)], axis=0)
    source = jnp.full((device_count * slot_most,), pair_count, jnp.int32)
    source = source.at[target].set(jnp.arange(pair_count, dtype=jnp.int32))
    owner = jnp.where(source < pair_count, source // topk, tok_rows)
    send_x = tokens_pad[owner].reshape(device_count, slot_most, width)
    send_g = scaled_pad[source].reshape(device_count, slot_most, hidden)
    return (send_x, send_g)


def sparse_body(tokens, grads, route_weights, route_ids, group_picks, frozen_up, factor_a, factor_b):
    tok_rows = tokens.shape[0]
    topk = route_ids.shape[1]
    width = tokens.shape[1]
    hidden = grads.shape[2]
    node_count = lax.axis_size("node")
    local_count = lax.axis_size("local")
    device_count = node_count * local_count
    group_size = device_count // GROUPS
    slot_most = 2 * (5 * tok_rows // 8) // group_size
    pair_count = tok_rows * topk
    frozen = frozen_up[0]
    first = factor_a[0]
    second = factor_b[0]
    experts = jnp.repeat(group_picks, 2, axis=1) * group_size + route_ids
    expert_flat = experts.reshape(-1)
    ranks = slot_ranks(expert_flat, device_count)
    target = expert_flat * slot_most + ranks
    scaled = (
        (grads.astype(jnp.float32) * route_weights[:, :, None])
        .astype(jnp.bfloat16)
        .reshape(pair_count, hidden)
    )
    send_x, send_g = send_buffers(tokens, scaled, target, device_count, slot_most)
    pieces = (
        lax.all_to_all(send_x, ("node", "local"), split_axis=0, concat_axis=0, tiled=True),
        lax.all_to_all(send_g, ("node", "local"), split_axis=0, concat_axis=0, tiled=True),
    )
    route_gradient, rank_space_rows, projected_rows = slot_grads(
        pieces[0], pieces[1], frozen, first, second
    )
    arrived, arrived_grads, route_gradient, rank_space_rows, projected_rows = (
        pieces[0],
        pieces[1],
        route_gradient,
        rank_space_rows,
        projected_rows,
    )
    input_rows = arrived.reshape(-1, width)
    gradient_rows = arrived_grads.reshape(-1, hidden)
    first_factor_gradient = (
        weight_gradient_total
        * adapter_scale_factor
        * lax.dot_general(
            input_rows,
            rank_space_rows.reshape(-1, rank_space_rows.shape[-1]),
            (((0,), (0,)), ((), ())),
            preferred_element_type=jnp.float32,
        )
    )
    second_factor_gradient = (
        weight_gradient_total
        * adapter_scale_factor
        * lax.dot_general(
            projected_rows.reshape(-1, projected_rows.shape[-1]),
            gradient_rows,
            (((0,), (0,)), ((), ())),
            preferred_element_type=jnp.float32,
        )
    )
    returned = lax.all_to_all(
        route_gradient, ("node", "local"), split_axis=0, concat_axis=0, tiled=True
    )
    picked = returned.reshape(-1, width)[target]
    input_grad = jnp.sum(picked.reshape(tok_rows, topk, width).astype(jnp.float32), axis=1).astype(
        jnp.bfloat16
    )
    return (input_grad, first_factor_gradient[None], second_factor_gradient[None])


MESH = pl.DeviceIdType.MESH


def tile_of(width):
    for tile in (512, 256, 128):
        if width % tile == 0:
            return tile
    return width


def visit_order(count):
    table = []
    for z in range(count):
        above, below = list(range(count - 1, z, -1)), list(range(z))
        order = []
        while above or below:
            first, other = (above, below) if len(above) >= len(below) else (below, above)
            order.append(first.pop(0))
            if other:
                order.append(other.pop(0))
        table.append(order + [z])
    return table


def return_kernel(
    z_count, send_ref, unpack_ref, frozen_ref, first_ref, second_ref, extra_ref,
    out_ref, fac_ref,
    arrived, part, summed, from_y, from_z, lhs, low,
    a_send, a_recv, extra_sem, c_send, c_recv, y_send, y_recv, z_send, z_recv,
):
    f32, bf16 = jnp.float32, jnp.bfloat16
    core = lax.axis_index("node")
    local = lax.axis_index("local")
    z, y = local // 2, lax.rem(local, 2)
    tok_rows = out_ref.shape[0]
    more = fac_ref.shape[0]
    width = out_ref.shape[1]
    tile = tile_of(width)
    nt = (((1,), (1,)), ((), ()))
    table = visit_order(z_count)

    core_peer = {"node": 1 - core}
    y_peer = {"local": z * 2 + 1 - y}

    device_count = 4 * z_count
    me = core * 2 * z_count + local
    barrier = pltpu.get_barrier_semaphore()

    @pl.loop(1, device_count)
    def _(step):
        flat = lax.rem(me + step, device_count)
        peer = {"node": flat // (2 * z_count), "local": lax.rem(flat, 2 * z_count)}
        pl.semaphore_signal(barrier, inc=1, device_id=peer, device_id_type=MESH)

    target = []
    for p in range(z_count):
        zt = jnp.int32(0)
        for i in range(z_count):
            zt = zt + jnp.where(z == i, table[i][p], 0)
        target.append(zt)

    extra_copies = []
    for p in range(z_count):
        copy = pltpu.make_async_copy(
            extra_ref.at[:, target[p]],
            part.at[target[p], :, :, pl.ds(tok_rows, more)],
            extra_sem.at[p],
        )
        copy.start()
        extra_copies.append(copy)

    def partner(p, i):
        other_core = core if i // 2 == 0 else 1 - core
        other_local = target[p] * 2 + (y if i % 2 == 0 else 1 - y)
        return other_core, other_local, other_core * 2 * z_count + other_local

    def a_copy(p, i):
        other_core, other_local, flat = partner(p, i)
        return pltpu.make_async_remote_copy(
            send_ref.at[flat], arrived.at[me], a_send.at[flat], a_recv.at[me],
            device_id={"node": other_core, "local": other_local}, device_id_type=MESH,
        )

    def a_arrival(p, i):
        _, _, flat = partner(p, i)
        return pltpu.make_async_remote_copy(
            send_ref.at[flat], arrived.at[flat], a_send.at[flat], a_recv.at[flat],
            device_id=core_peer, device_id_type=MESH,
        )

    own_rows = pltpu.make_async_copy(send_ref.at[me], arrived.at[me], a_recv.at[me])
    own_rows.start()
    exchanged = [(p, i) for p in range(z_count) for i in range(4) if (p, i) != (z_count - 1, 0)]
    pl.semaphore_wait(barrier, device_count - 1)
    for p, i in exchanged:
        a_copy(p, i).start()

    def compute(p):
        zt = target[p]
        for i in range(4):
            if (p, i) in exchanged:
                a_arrival(p, i).wait_recv()
            else:
                own_rows.wait()
        for i in range(4):
            origin = (i // 2) * 2 * z_count + zt * 2 + i % 2
            rows = jnp.dot(unpack_ref[origin], arrived[origin], preferred_element_type=f32)
            lhs[pl.ds(i * tok_rows, tok_rows), :] = rows.astype(bf16)
        low[...] = lax.dot_general(
            lhs[...], second_ref[...], nt, preferred_element_type=f32
        ).astype(bf16)

        @pl.loop(0, width // tile)
        def _(j):
            columns = pl.ds(pl.multiple_of(j * tile, tile), tile)
            value = lax.dot_general(
                lhs[...], frozen_ref[columns, :], nt, preferred_element_type=f32
            ) + lax.dot_general(low[...], first_ref[columns, :], nt, preferred_element_type=f32)
            value = value.astype(bf16)
            for i in range(4):
                part[zt, i // 2, i % 2, pl.ds(0, tok_rows), columns] = value[
                    i * tok_rows : (i + 1) * tok_rows
                ]

        extra_copies[p].wait()

    def c_copy(p):
        return pltpu.make_async_remote_copy(
            part.at[target[p], 1 - core], summed.at[target[p]], c_send.at[p], c_recv.at[p],
            device_id=core_peer, device_id_type=MESH,
        )

    def y_copy(p):
        return pltpu.make_async_remote_copy(
            summed.at[target[p], 1 - y], from_y.at[target[p]], y_send.at[p], y_recv.at[p],
            device_id=y_peer, device_id_type=MESH,
        )

    def over_rows(count, step):
        @pl.loop(0, count // 16)
        def _(i):
            step(pl.ds(pl.multiple_of(i * 16, 16), 16))

    def add_core(p):
        zt = target[p]
        c_copy(p).wait_recv()
        for half in (1 - y, y):

            def step(rows):
                summed[zt, half, rows, :] = (
                    summed[zt, half, rows, :].astype(f32) + part[zt, core, half, rows, :].astype(f32)
                ).astype(bf16)

            over_rows(tok_rows + more, step)
            if half is not y:
                y_copy(p).start()

    compute(0)
    c_copy(0).start()
    for p in range(1, z_count):
        compute(p)
        c_copy(p).start()
        add_core(p - 1)
    add_core(z_count - 1)

    def z_copy(p, slot, peer):
        return pltpu.make_async_remote_copy(
            summed.at[target[p], y], from_z.at[slot], z_send.at[p], z_recv.at[slot],
            device_id={"local": peer}, device_id_type=MESH,
        )

    def slot_wait(slot):
        z_copy(0, slot, local).wait_recv()

    for p in range(z_count - 1):
        zt = target[p]
        up = zt > z
        y_copy(p).wait_recv()
        passing = jnp.logical_or(jnp.logical_and(up, z > 0), jnp.logical_and(zt < z, z < z_count - 1))

        @pl.when(passing)
        def _():
            slot_wait(zt)

            def step(rows):
                summed[zt, y, rows, :] = (
                    summed[zt, y, rows, :].astype(f32)
                    + from_y[zt, rows, :].astype(f32)
                    + from_z[zt, rows, :].astype(f32)
                ).astype(bf16)

            over_rows(tok_rows + more, step)

        @pl.when(jnp.logical_not(passing))
        def _():
            def step(rows):
                summed[zt, y, rows, :] = (
                    summed[zt, y, rows, :].astype(f32) + from_y[zt, rows, :].astype(f32)
                ).astype(bf16)

            over_rows(tok_rows + more, step)

        slot = jnp.where(zt == z - 1, z_count, zt)
        z_copy(p, slot, jnp.where(up, local + 2, local - 2)).start()

    p = z_count - 1
    y_copy(p).wait_recv()

    def finish(with_below, with_above):
        def total(rows):
            value = summed[z, y, rows, :].astype(f32) + from_y[z, rows, :].astype(f32)
            if with_below:
                value = value + from_z[z, rows, :].astype(f32)
            if with_above:
                value = value + from_z[z_count, rows, :].astype(f32)
            return value

        if with_below:
            slot_wait(z)
        if with_above:
            slot_wait(z_count)

        def step(rows):
            out_ref[rows, :] = total(rows).astype(bf16)

        over_rows(tok_rows, step)
        for start in range(0, more, 16):
            fac_ref[pl.ds(start, 16), :] = total(pl.ds(tok_rows + start, 16))

    @pl.when(z == 0)
    def _():
        finish(False, True)

    @pl.when(z == z_count - 1)
    def _():
        finish(True, False)

    @pl.when(jnp.logical_and(z > 0, z < z_count - 1))
    def _():
        finish(True, True)

    for p, i in exchanged:
        a_copy(p, i).wait_send()
    for p in range(z_count):
        c_copy(p).wait_send()
        y_copy(p).wait_send()
    for p in range(z_count - 1):
        z_copy(p, 0, local).wait_send()


def return_sums(send_g, unpack, frozen, first, second, extra, tok_rows):
    bf16 = jnp.bfloat16
    z_count, more, width = extra.shape[1], extra.shape[3], extra.shape[4]
    rows = tok_rows + more
    dma = pltpu.SemaphoreType.DMA
    vmem = pl.BlockSpec(memory_space=pltpu.VMEM)
    routes = 4 * z_count * tok_rows
    return pl.pallas_call(
        functools.partial(return_kernel, z_count),
        out_shape=(
            jax.ShapeDtypeStruct((tok_rows, width), bf16),
            jax.ShapeDtypeStruct((more, width), jnp.float32),
        ),
        in_specs=[pl.BlockSpec(memory_space=pl.ANY)] + [vmem] * 4 + [pl.BlockSpec(memory_space=pl.ANY)],
        out_specs=(vmem, vmem),
        scratch_shapes=[
            pltpu.VMEM(send_g.shape, bf16),
            pltpu.VMEM((z_count, 2, 2, rows, width), bf16),
            pltpu.VMEM((z_count, 2, rows, width), bf16),
            pltpu.VMEM((z_count, rows, width), bf16),
            pltpu.VMEM((z_count + 1, rows, width), bf16),
            pltpu.VMEM((4 * tok_rows, frozen.shape[1]), bf16),
            pltpu.VMEM((4 * tok_rows, second.shape[0]), bf16),
            dma((4 * z_count,)), dma((4 * z_count,)),
            dma((z_count,)), dma((z_count,)), dma((z_count,)), dma((z_count,)),
            dma((z_count,)), dma((z_count,)), dma((z_count + 1,)),
        ],
        compiler_params=pltpu.CompilerParams(
            collective_id=0, has_side_effects=True, vmem_limit_bytes=60 * 2**20
        ),
        cost_estimate=pl.CostEstimate(
            flops=2 * routes * width * frozen.shape[1], bytes_accessed=20 * 2**20, transcendentals=0
        ),
    )(send_g, unpack, frozen, first, second, extra)


def gather_kernel(z_count, own_ref, all_ref, own_sem, recv, up_send, down_send, y_send, c_send):
    core = lax.axis_index("node")
    local = lax.axis_index("local")
    z, y = local // 2, lax.rem(local, 2)
    core_peer = {"node": 1 - core}
    y_peer = {"local": z * 2 + 1 - y}
    above, below = {"local": local + 2}, {"local": local - 2}
    has_above, has_below = z < z_count - 1, z > 0

    barrier = pltpu.get_barrier_semaphore()
    pl.semaphore_signal(barrier, inc=1, device_id=core_peer, device_id_type=MESH)
    pl.semaphore_signal(barrier, inc=1, device_id=y_peer, device_id_type=MESH)

    @pl.when(has_below)
    def _():
        pl.semaphore_signal(barrier, inc=1, device_id=below, device_id_type=MESH)

    @pl.when(has_above)
    def _():
        pl.semaphore_signal(barrier, inc=1, device_id=above, device_id_type=MESH)

    place = pltpu.make_async_copy(own_ref, all_ref.at[core, z, y], own_sem)
    place.start()
    place.wait()
    neighbours = 2 + jnp.where(has_below, 1, 0) + jnp.where(has_above, 1, 0)
    pl.semaphore_wait(barrier, neighbours)

    def copy(zs, ys, send_sem, peer):
        return pltpu.make_async_remote_copy(
            all_ref.at[core, zs, ys], all_ref.at[core, zs, ys], send_sem, recv.at[core, zs, ys],
            device_id=peer, device_id_type=MESH,
        )

    def arrival(cs, zs, ys):
        pltpu.make_async_remote_copy(
            all_ref.at[cs, zs, ys], all_ref.at[cs, zs, ys], own_sem, recv.at[cs, zs, ys],
            device_id=core_peer, device_id_type=MESH,
        ).wait_recv()

    def spread(zs):
        copy(zs, y, y_send.at[zs], y_peer).start()
        copy(zs, y, c_send.at[zs, y], core_peer).start()

    @pl.when(has_above)
    def _():
        copy(z, y, up_send.at[z], above).start()

    @pl.when(has_below)
    def _():
        copy(z, y, down_send.at[z], below).start()

    spread(z)
    for distance in range(1, z_count):

        @pl.when(z - distance >= 0)
        def _():
            zs = z - distance
            arrival(core, zs, y)

            @pl.when(has_above)
            def _():
                copy(zs, y, up_send.at[zs], above).start()

            spread(zs)

        @pl.when(z + distance < z_count)
        def _():
            zs = z + distance
            arrival(core, zs, y)

            @pl.when(has_below)
            def _():
                copy(zs, y, down_send.at[zs], below).start()

            spread(zs)

    def from_y(zs):
        arrival(core, zs, 1 - y)
        copy(zs, 1 - y, c_send.at[zs, 1 - y], core_peer).start()

    from_y(z)
    for distance in range(1, z_count):

        @pl.when(z - distance >= 0)
        def _():
            from_y(z - distance)

        @pl.when(z + distance < z_count)
        def _():
            from_y(z + distance)

    for zs in range(z_count):
        for ys in range(2):
            arrival(1 - core, zs, ys)
            copy(zs, ys, c_send.at[zs, ys], core_peer).wait_send()
        copy(zs, y, y_send.at[zs], y_peer).wait_send()

        @pl.when(jnp.logical_and(has_above, zs <= z))
        def _():
            copy(zs, y, up_send.at[zs], core_peer).wait_send()

        @pl.when(jnp.logical_and(has_below, zs >= z))
        def _():
            copy(zs, y, down_send.at[zs], core_peer).wait_send()


def gather_shards(own, device_count):
    z_count = device_count // 4
    dma = pltpu.SemaphoreType.DMA
    vmem = pl.BlockSpec(memory_space=pltpu.VMEM)
    gathered = pl.pallas_call(
        functools.partial(gather_kernel, z_count),
        out_shape=jax.ShapeDtypeStruct((2, z_count, 2) + own.shape, own.dtype),
        in_specs=[vmem],
        out_specs=vmem,
        scratch_shapes=[
            dma, dma((2, z_count, 2)), dma((z_count,)), dma((z_count,)),
            dma((z_count,)), dma((z_count, 2)),
        ],
        compiler_params=pltpu.CompilerParams(
            collective_id=1, has_side_effects=True, vmem_limit_bytes=24 * 2**20
        ),
        cost_estimate=pl.CostEstimate(flops=0, bytes_accessed=100 * 2**20, transcendentals=0),
    )(own)
    return gathered.reshape((device_count * own.shape[0],) + own.shape[1:])


def scale_routes(grads, route_weights):
    pair_count = grads.shape[0] * grads.shape[1]
    return (
        (grads.astype(jnp.float32) * route_weights[:, :, None])
        .astype(jnp.bfloat16)
        .reshape(pair_count, grads.shape[2])
    )


def dense_body(tokens, grads, route_weights, route_ids, group_picks, frozen_up, factor_a, factor_b):
    tok_rows, width = tokens.shape
    topk = route_ids.shape[1]
    hidden = grads.shape[2]
    rank = factor_b.shape[1]
    axes = ("node", "local")
    device_count = lax.axis_size("node") * lax.axis_size("local")
    me = lax.axis_index("node") * lax.axis_size("local") + lax.axis_index("local")
    group_size = device_count // GROUPS
    slot_most = 2 * (5 * tok_rows // 8) // group_size
    f32, bf16 = jnp.float32, jnp.bfloat16
    experts = jnp.repeat(group_picks, 2, axis=1) * group_size + route_ids
    expert_flat = experts.reshape(-1)
    first_t = factor_a[0].T
    second = factor_b[0]
    table = jnp.zeros((rank, tok_rows), bf16).at[:topk].set(experts.T.astype(bf16))
    ids = jnp.arange(device_count, dtype=jnp.int32)
    member = (experts[:, :, None] == ids[None, None, :]).any(axis=1)
    order = jnp.cumsum(member.astype(jnp.int32), axis=0) - 1
    ranks = jnp.sum(jnp.where(experts[:, :, None] == ids, order[:, None, :], 0), axis=2)
    target = experts * slot_most + ranks
    scaled = scale_routes(grads, route_weights)
    slots = jnp.arange(device_count * slot_most, dtype=jnp.int32)
    pack = (target.reshape(1, -1) == slots[:, None]).astype(bf16)
    send_g = jnp.dot(pack, scaled, preferred_element_type=f32).astype(bf16)
    send_g = send_g.reshape(device_count, slot_most, hidden)
    own = jnp.concatenate([first_t, second, table], axis=1)
    shared = gather_shards(own, device_count)
    all_first = shared[:, :width]
    all_second = shared[:, width : width + hidden]
    tables = shared[:, width + hidden :].reshape(device_count, rank, tok_rows)[:, :topk]

    owner_mask = expert_flat[:, None] == jnp.repeat(ids, rank)[None, :]
    middle = lax.dot_general(scaled, all_second, (((1,), (1,)), ((), ())), preferred_element_type=f32)
    middle = jnp.where(owner_mask, middle, 0.0).reshape(tok_rows, topk, -1).sum(axis=1).astype(bf16)
    projected = lax.dot_general(
        tokens, all_first, (((1,), (1,)), ((), ())), preferred_element_type=f32
    ).astype(bf16)
    projected = jnp.where(
        owner_mask.reshape(tok_rows, topk, -1), projected[:, None, :], jnp.zeros((), bf16)
    ).reshape(tok_rows * topk, -1)
    share_a = lax.dot_general(middle, tokens, (((0,), (0,)), ((), ())), preferred_element_type=f32)
    share_b = lax.dot_general(projected, scaled, (((0,), (0,)), ((), ())), preferred_element_type=f32)
    half = rank // 2
    share_b = share_b.astype(bf16).reshape(device_count, 2, half, hidden)
    share_b = jnp.concatenate([share_b[:, 0], share_b[:, 1]], axis=2)
    share_b = jnp.pad(share_b, ((0, 0), (0, 0), (0, width - 2 * hidden)))
    extra = jnp.concatenate(
        [share_a.astype(bf16).reshape(device_count, rank, width), share_b], axis=1
    ).reshape(2, device_count // 4, 2, rank + half, width)

    mine = (tables == me.astype(bf16)).any(axis=1)
    place = jnp.cumsum(mine.astype(jnp.int32), axis=1) - 1
    unpack = (
        mine[:, :, None] & (place[:, :, None] == jnp.arange(slot_most, dtype=jnp.int32))
    ).astype(bf16)
    input_grad, factor_sums = return_sums(
        send_g, unpack, frozen_up[0], factor_a[0] * adapter_scale_factor, second, extra, tok_rows
    )
    factor_sums = factor_sums * (weight_gradient_total * adapter_scale_factor)
    grad_a = factor_sums[:rank].T[None]
    last = factor_sums[rank:]
    grad_b = jnp.concatenate([last[:, :hidden], last[:, hidden : 2 * hidden]], axis=0)[None]
    return (input_grad, grad_a, grad_b)


def body(tokens, grads, route_weights, route_ids, group_picks, frozen_up, factor_a, factor_b):
    tok_rows = tokens.shape[0]
    group_size = lax.axis_size("node") * lax.axis_size("local") // GROUPS
    slot_most = 2 * (5 * tok_rows // 8) // group_size
    plan = dense_body if tok_rows <= 2 * slot_most else sparse_body
    return plan(tokens, grads, route_weights, route_ids, group_picks, frozen_up, factor_a, factor_b)


def solution(mesh):
    return jax.shard_map(
        body,
        mesh=mesh,
        in_specs=(
            P(("rep", "node", "local"), None),
            P(("rep", "node", "local"), None, None),
            P(("rep", "node", "local"), None),
            P(("rep", "node", "local"), None),
            P(("rep", "node", "local"), None),
            P(("node", "local"), None, None),
            P(("node", "local"), None, None),
            P(("node", "local"), None, None),
        ),
        out_specs=(
            P(("rep", "node", "local"), None),
            P(("rep", "node", "local"), None, None),
            P(("rep", "node", "local"), None, None),
        ),
        check_vma=False,
    )
```

```python
import functools
import jax
import jax.numpy as jnp
from jax import lax
from jax.experimental import pallas as pl
from jax.experimental.pallas import tpu as pltpu
from jax.sharding import PartitionSpec as P

GROUPS = 8


adapter_scale_factor = 0.25
weight_gradient_total = 1.0 / 32.0


def slot_ranks(expert_flat, device_count):
    onehot = (expert_flat[:, None] == jnp.arange(device_count, dtype=jnp.int32)[None, :]).astype(
        jnp.int32
    )
    earlier = jnp.cumsum(onehot, axis=0) - onehot
    return jnp.sum(earlier * onehot, axis=1)


def slot_grads(arrived, arrived_grads, frozen, first, second):
    lead = arrived.shape[:-1]
    input_rows = arrived.reshape(-1, arrived.shape[-1])
    gradient_rows = arrived_grads.reshape(-1, arrived_grads.shape[-1])
    rank_space_rows = lax.dot_general(
        gradient_rows, second, (((1,), (1,)), ((), ())), preferred_element_type=jnp.float32
    ).astype(jnp.bfloat16)
    joined_rows = jnp.concatenate([gradient_rows, rank_space_rows], axis=1)
    joined_weight = jnp.concatenate([frozen, first * adapter_scale_factor], axis=1)
    route_gradient = lax.dot_general(
        joined_rows, joined_weight, (((1,), (1,)), ((), ())), preferred_element_type=jnp.float32
    ).astype(jnp.bfloat16)
    projected_rows = jnp.dot(input_rows, first, preferred_element_type=jnp.float32).astype(
        jnp.bfloat16
    )
    return (
        route_gradient.reshape(lead + (frozen.shape[0],)),
        rank_space_rows.reshape(lead + (second.shape[0],)),
        projected_rows.reshape(lead + (second.shape[0],)),
    )


def send_buffers(tokens, scaled, target, device_count, slot_most):
    tok_rows, width = tokens.shape
    pair_count, hidden = scaled.shape
    topk = pair_count // tok_rows
    scaled_pad = jnp.concatenate([scaled, jnp.zeros((1, hidden), jnp.bfloat16)], axis=0)
    tokens_pad = jnp.concatenate([tokens, jnp.zeros((1, width), jnp.bfloat16)], axis=0)
    source = jnp.full((device_count * slot_most,), pair_count, jnp.int32)
    source = source.at[target].set(jnp.arange(pair_count, dtype=jnp.int32))
    owner = jnp.where(source < pair_count, source // topk, tok_rows)
    send_x = tokens_pad[owner].reshape(device_count, slot_most, width)
    send_g = scaled_pad[source].reshape(device_count, slot_most, hidden)
    return (send_x, send_g)


def sparse_body(tokens, grads, route_weights, route_ids, group_picks, frozen_up, factor_a, factor_b):
    tok_rows = tokens.shape[0]
    topk = route_ids.shape[1]
    width = tokens.shape[1]
    hidden = grads.shape[2]
    node_count = lax.axis_size("node")
    local_count = lax.axis_size("local")
    device_count = node_count * local_count
    group_size = device_count // GROUPS
    slot_most = 2 * (5 * tok_rows // 8) // group_size
    pair_count = tok_rows * topk
    frozen = frozen_up[0]
    first = factor_a[0]
    second = factor_b[0]
    experts = jnp.repeat(group_picks, 2, axis=1) * group_size + route_ids
    expert_flat = experts.reshape(-1)
    ranks = slot_ranks(expert_flat, device_count)
    target = expert_flat * slot_most + ranks
    scaled = (
        (grads.astype(jnp.float32) * route_weights[:, :, None])
        .astype(jnp.bfloat16)
        .reshape(pair_count, hidden)
    )
    send_x, send_g = send_buffers(tokens, scaled, target, device_count, slot_most)
    pieces = (
        lax.all_to_all(send_x, ("node", "local"), split_axis=0, concat_axis=0, tiled=True),
        lax.all_to_all(send_g, ("node", "local"), split_axis=0, concat_axis=0, tiled=True),
    )
    route_gradient, rank_space_rows, projected_rows = slot_grads(
        pieces[0], pieces[1], frozen, first, second
    )
    arrived, arrived_grads, route_gradient, rank_space_rows, projected_rows = (
        pieces[0],
        pieces[1],
        route_gradient,
        rank_space_rows,
        projected_rows,
    )
    input_rows = arrived.reshape(-1, width)
    gradient_rows = arrived_grads.reshape(-1, hidden)
    first_factor_gradient = (
        weight_gradient_total
        * adapter_scale_factor
        * lax.dot_general(
            input_rows,
            rank_space_rows.reshape(-1, rank_space_rows.shape[-1]),
            (((0,), (0,)), ((), ())),
            preferred_element_type=jnp.float32,
        )
    )
    second_factor_gradient = (
        weight_gradient_total
        * adapter_scale_factor
        * lax.dot_general(
            projected_rows.reshape(-1, projected_rows.shape[-1]),
            gradient_rows,
            (((0,), (0,)), ((), ())),
            preferred_element_type=jnp.float32,
        )
    )
    returned = lax.all_to_all(
        route_gradient, ("node", "local"), split_axis=0, concat_axis=0, tiled=True
    )
    picked = returned.reshape(-1, width)[target]
    input_grad = jnp.sum(picked.reshape(tok_rows, topk, width).astype(jnp.float32), axis=1).astype(
        jnp.bfloat16
    )
    return (input_grad, first_factor_gradient[None], second_factor_gradient[None])


MESH = pl.DeviceIdType.MESH


def tile_of(width):
    for tile in (512, 256, 128):
        if width % tile == 0:
            return tile
    return width


def visit_order(count):
    table = []
    for z in range(count):
        above, below = list(range(count - 1, z, -1)), list(range(z))
        order = []
        while above or below:
            first, other = (above, below) if len(above) >= len(below) else (below, above)
            order.append(first.pop(0))
            if other:
                order.append(other.pop(0))
        table.append(order + [z])
    return table


def return_kernel(
    z_count, send_ref, unpack_ref, frozen_ref, first_ref, second_ref, extra_ref,
    out_ref, fac_ref,
    arrived, part, summed, from_y, from_z, lhs, low,
    a_send, a_recv, extra_sem, c_send, c_recv, y_send, y_recv, z_send, z_recv,
):
    f32, bf16 = jnp.float32, jnp.bfloat16
    core = lax.axis_index("node")
    local = lax.axis_index("local")
    z, y = local // 2, lax.rem(local, 2)
    tok_rows = out_ref.shape[0]
    more = fac_ref.shape[0]
    width = out_ref.shape[1]
    tile = tile_of(width)
    nt = (((1,), (1,)), ((), ()))
    table = visit_order(z_count)

    core_peer = {"node": 1 - core}
    y_peer = {"local": z * 2 + 1 - y}

    device_count = 4 * z_count
    me = core * 2 * z_count + local
    barrier = pltpu.get_barrier_semaphore()

    @pl.loop(1, device_count)
    def _(step):
        flat = lax.rem(me + step, device_count)
        peer = {"node": flat // (2 * z_count), "local": lax.rem(flat, 2 * z_count)}
        pl.semaphore_signal(barrier, inc=1, device_id=peer, device_id_type=MESH)

    target = []
    for p in range(z_count):
        zt = jnp.int32(0)
        for i in range(z_count):
            zt = zt + jnp.where(z == i, table[i][p], 0)
        target.append(zt)

    extra_copies = []
    for p in range(z_count):
        copy = pltpu.make_async_copy(
            extra_ref.at[:, target[p]],
            part.at[target[p], :, :, pl.ds(tok_rows, more)],
            extra_sem.at[p],
        )
        copy.start()
        extra_copies.append(copy)

    def partner(p, i):
        other_core = core if i // 2 == 0 else 1 - core
        other_local = target[p] * 2 + (y if i % 2 == 0 else 1 - y)
        return other_core, other_local, other_core * 2 * z_count + other_local

    def a_copy(p, i):
        other_core, other_local, flat = partner(p, i)
        return pltpu.make_async_remote_copy(
            send_ref.at[flat], arrived.at[me], a_send.at[flat], a_recv.at[me],
            device_id={"node": other_core, "local": other_local}, device_id_type=MESH,
        )

    def a_arrival(p, i):
        _, _, flat = partner(p, i)
        return pltpu.make_async_remote_copy(
            send_ref.at[flat], arrived.at[flat], a_send.at[flat], a_recv.at[flat],
            device_id=core_peer, device_id_type=MESH,
        )

    own_rows = pltpu.make_async_copy(send_ref.at[me], arrived.at[me], a_recv.at[me])
    own_rows.start()
    exchanged = [(p, i) for p in range(z_count) for i in range(4) if (p, i) != (z_count - 1, 0)]
    pl.semaphore_wait(barrier, device_count - 1)

    def send_rows(p):
        for i in range(4):
            if (p, i) in exchanged:
                a_copy(p, i).start()

    send_rows(0)
    for i in range(4):
        if (0, i) in exchanged:
            a_copy(0, i).wait_send()
    if z_count > 1:
        send_rows(1)

    def compute(p):
        zt = target[p]
        for i in range(4):
            if (p, i) in exchanged:
                a_arrival(p, i).wait_recv()
            else:
                own_rows.wait()
        if p == 0:
            for later in range(2, z_count):
                send_rows(later)
        for i in range(4):
            origin = (i // 2) * 2 * z_count + zt * 2 + i % 2
            rows = jnp.dot(unpack_ref[origin], arrived[origin], preferred_element_type=f32)
            lhs[pl.ds(i * tok_rows, tok_rows), :] = rows.astype(bf16)
        low[...] = lax.dot_general(
            lhs[...], second_ref[...], nt, preferred_element_type=f32
        ).astype(bf16)

        @pl.loop(0, width // tile)
        def _(j):
            columns = pl.ds(pl.multiple_of(j * tile, tile), tile)
            value = lax.dot_general(
                lhs[...], frozen_ref[columns, :], nt, preferred_element_type=f32
            ) + lax.dot_general(low[...], first_ref[columns, :], nt, preferred_element_type=f32)
            value = value.astype(bf16)
            for i in range(4):
                part[zt, i // 2, i % 2, pl.ds(0, tok_rows), columns] = value[
                    i * tok_rows : (i + 1) * tok_rows
                ]

        extra_copies[p].wait()

    def c_copy(p):
        return pltpu.make_async_remote_copy(
            part.at[target[p], 1 - core], summed.at[target[p]], c_send.at[p], c_recv.at[p],
            device_id=core_peer, device_id_type=MESH,
        )

    def y_copy(p):
        return pltpu.make_async_remote_copy(
            summed.at[target[p], 1 - y], from_y.at[target[p]], y_send.at[p], y_recv.at[p],
            device_id=y_peer, device_id_type=MESH,
        )

    def over_rows(count, step):
        @pl.loop(0, count // 16)
        def _(i):
            step(pl.ds(pl.multiple_of(i * 16, 16), 16))

    def add_core(p):
        zt = target[p]
        c_copy(p).wait_recv()
        for half in (1 - y, y):

            def step(rows):
                summed[zt, half, rows, :] = (
                    summed[zt, half, rows, :].astype(f32) + part[zt, core, half, rows, :].astype(f32)
                ).astype(bf16)

            over_rows(tok_rows + more, step)
            if half is not y:
                y_copy(p).start()

    compute(0)
    c_copy(0).start()
    for p in range(1, z_count):
        compute(p)
        c_copy(p).start()
        add_core(p - 1)
    add_core(z_count - 1)

    def z_copy(p, slot, peer):
        return pltpu.make_async_remote_copy(
            summed.at[target[p], y], from_z.at[slot], z_send.at[p], z_recv.at[slot],
            device_id={"local": peer}, device_id_type=MESH,
        )

    def slot_wait(slot):
        z_copy(0, slot, local).wait_recv()

    for p in range(z_count - 1):
        zt = target[p]
        up = zt > z
        y_copy(p).wait_recv()
        passing = jnp.logical_or(jnp.logical_and(up, z > 0), jnp.logical_and(zt < z, z < z_count - 1))

        @pl.when(passing)
        def _():
            slot_wait(zt)

            def step(rows):
                summed[zt, y, rows, :] = (
                    summed[zt, y, rows, :].astype(f32)
                    + from_y[zt, rows, :].astype(f32)
                    + from_z[zt, rows, :].astype(f32)
                ).astype(bf16)

            over_rows(tok_rows + more, step)

        @pl.when(jnp.logical_not(passing))
        def _():
            def step(rows):
                summed[zt, y, rows, :] = (
                    summed[zt, y, rows, :].astype(f32) + from_y[zt, rows, :].astype(f32)
                ).astype(bf16)

            over_rows(tok_rows + more, step)

        slot = jnp.where(zt == z - 1, z_count, zt)
        z_copy(p, slot, jnp.where(up, local + 2, local - 2)).start()

    p = z_count - 1
    y_copy(p).wait_recv()

    def finish(with_below, with_above):
        def total(rows):
            value = summed[z, y, rows, :].astype(f32) + from_y[z, rows, :].astype(f32)
            if with_below:
                value = value + from_z[z, rows, :].astype(f32)
            if with_above:
                value = value + from_z[z_count, rows, :].astype(f32)
            return value

        if with_below:
            slot_wait(z)
        if with_above:
            slot_wait(z_count)

        def step(rows):
            out_ref[rows, :] = total(rows).astype(bf16)

        over_rows(tok_rows, step)
        for start in range(0, more, 16):
            fac_ref[pl.ds(start, 16), :] = total(pl.ds(tok_rows + start, 16))

    @pl.when(z == 0)
    def _():
        finish(False, True)

    @pl.when(z == z_count - 1)
    def _():
        finish(True, False)

    @pl.when(jnp.logical_and(z > 0, z < z_count - 1))
    def _():
        finish(True, True)

    for p, i in exchanged:
        if p > 0:
            a_copy(p, i).wait_send()
    for p in range(z_count):
        c_copy(p).wait_send()
        y_copy(p).wait_send()
    for p in range(z_count - 1):
        z_copy(p, 0, local).wait_send()


def return_sums(send_g, unpack, frozen, first, second, extra, tok_rows):
    bf16 = jnp.bfloat16
    z_count, more, width = extra.shape[1], extra.shape[3], extra.shape[4]
    rows = tok_rows + more
    dma = pltpu.SemaphoreType.DMA
    vmem = pl.BlockSpec(memory_space=pltpu.VMEM)
    routes = 4 * z_count * tok_rows
    return pl.pallas_call(
        functools.partial(return_kernel, z_count),
        out_shape=(
            jax.ShapeDtypeStruct((tok_rows, width), bf16),
            jax.ShapeDtypeStruct((more, width), jnp.float32),
        ),
        in_specs=[pl.BlockSpec(memory_space=pl.ANY)] + [vmem] * 4 + [pl.BlockSpec(memory_space=pl.ANY)],
        out_specs=(vmem, vmem),
        scratch_shapes=[
            pltpu.VMEM(send_g.shape, bf16),
            pltpu.VMEM((z_count, 2, 2, rows, width), bf16),
            pltpu.VMEM((z_count, 2, rows, width), bf16),
            pltpu.VMEM((z_count, rows, width), bf16),
            pltpu.VMEM((z_count + 1, rows, width), bf16),
            pltpu.VMEM((4 * tok_rows, frozen.shape[1]), bf16),
            pltpu.VMEM((4 * tok_rows, second.shape[0]), bf16),
            dma((4 * z_count,)), dma((4 * z_count,)),
            dma((z_count,)), dma((z_count,)), dma((z_count,)), dma((z_count,)),
            dma((z_count,)), dma((z_count,)), dma((z_count + 1,)),
        ],
        compiler_params=pltpu.CompilerParams(
            collective_id=0, has_side_effects=True, vmem_limit_bytes=60 * 2**20
        ),
        cost_estimate=pl.CostEstimate(
            flops=2 * routes * width * frozen.shape[1], bytes_accessed=20 * 2**20, transcendentals=0
        ),
    )(send_g, unpack, frozen, first, second, extra)


def gather_kernel(z_count, own_ref, all_ref, own_sem, recv, up_send, down_send, y_send, c_send):
    core = lax.axis_index("node")
    local = lax.axis_index("local")
    z, y = local // 2, lax.rem(local, 2)
    core_peer = {"node": 1 - core}
    y_peer = {"local": z * 2 + 1 - y}
    above, below = {"local": local + 2}, {"local": local - 2}
    has_above, has_below = z < z_count - 1, z > 0

    barrier = pltpu.get_barrier_semaphore()
    pl.semaphore_signal(barrier, inc=1, device_id=core_peer, device_id_type=MESH)
    pl.semaphore_signal(barrier, inc=1, device_id=y_peer, device_id_type=MESH)

    @pl.when(has_below)
    def _():
        pl.semaphore_signal(barrier, inc=1, device_id=below, device_id_type=MESH)

    @pl.when(has_above)
    def _():
        pl.semaphore_signal(barrier, inc=1, device_id=above, device_id_type=MESH)

    place = pltpu.make_async_copy(own_ref, all_ref.at[core, z, y], own_sem)
    place.start()
    place.wait()
    neighbours = 2 + jnp.where(has_below, 1, 0) + jnp.where(has_above, 1, 0)
    pl.semaphore_wait(barrier, neighbours)

    def copy(zs, ys, send_sem, peer):
        return pltpu.make_async_remote_copy(
            all_ref.at[core, zs, ys], all_ref.at[core, zs, ys], send_sem, recv.at[core, zs, ys],
            device_id=peer, device_id_type=MESH,
        )

    def arrival(cs, zs, ys):
        pltpu.make_async_remote_copy(
            all_ref.at[cs, zs, ys], all_ref.at[cs, zs, ys], own_sem, recv.at[cs, zs, ys],
            device_id=core_peer, device_id_type=MESH,
        ).wait_recv()

    def spread(zs):
        copy(zs, y, y_send.at[zs], y_peer).start()
        copy(zs, y, c_send.at[zs, y], core_peer).start()

    @pl.when(has_above)
    def _():
        copy(z, y, up_send.at[z], above).start()

    @pl.when(has_below)
    def _():
        copy(z, y, down_send.at[z], below).start()

    spread(z)
    for distance in range(1, z_count):

        @pl.when(z - distance >= 0)
        def _():
            zs = z - distance
            arrival(core, zs, y)

            @pl.when(has_above)
            def _():
                copy(zs, y, up_send.at[zs], above).start()

            spread(zs)

        @pl.when(z + distance < z_count)
        def _():
            zs = z + distance
            arrival(core, zs, y)

            @pl.when(has_below)
            def _():
                copy(zs, y, down_send.at[zs], below).start()

            spread(zs)

    def from_y(zs):
        arrival(core, zs, 1 - y)
        copy(zs, 1 - y, c_send.at[zs, 1 - y], core_peer).start()

    from_y(z)
    for distance in range(1, z_count):

        @pl.when(z - distance >= 0)
        def _():
            from_y(z - distance)

        @pl.when(z + distance < z_count)
        def _():
            from_y(z + distance)

    for zs in range(z_count):
        for ys in range(2):
            arrival(1 - core, zs, ys)
            copy(zs, ys, c_send.at[zs, ys], core_peer).wait_send()
        copy(zs, y, y_send.at[zs], y_peer).wait_send()

        @pl.when(jnp.logical_and(has_above, zs <= z))
        def _():
            copy(zs, y, up_send.at[zs], core_peer).wait_send()

        @pl.when(jnp.logical_and(has_below, zs >= z))
        def _():
            copy(zs, y, down_send.at[zs], core_peer).wait_send()


def gather_shards(own, device_count):
    z_count = device_count // 4
    dma = pltpu.SemaphoreType.DMA
    vmem = pl.BlockSpec(memory_space=pltpu.VMEM)
    gathered = pl.pallas_call(
        functools.partial(gather_kernel, z_count),
        out_shape=jax.ShapeDtypeStruct((2, z_count, 2) + own.shape, own.dtype),
        in_specs=[vmem],
        out_specs=vmem,
        scratch_shapes=[
            dma, dma((2, z_count, 2)), dma((z_count,)), dma((z_count,)),
            dma((z_count,)), dma((z_count, 2)),
        ],
        compiler_params=pltpu.CompilerParams(
            collective_id=1, has_side_effects=True, vmem_limit_bytes=24 * 2**20
        ),
        cost_estimate=pl.CostEstimate(flops=0, bytes_accessed=100 * 2**20, transcendentals=0),
    )(own)
    return gathered.reshape((device_count * own.shape[0],) + own.shape[1:])


def scale_routes(grads, route_weights):
    pair_count = grads.shape[0] * grads.shape[1]
    return (
        (grads.astype(jnp.float32) * route_weights[:, :, None])
        .astype(jnp.bfloat16)
        .reshape(pair_count, grads.shape[2])
    )


def dense_body(tokens, grads, route_weights, route_ids, group_picks, frozen_up, factor_a, factor_b):
    tok_rows, width = tokens.shape
    topk = route_ids.shape[1]
    hidden = grads.shape[2]
    rank = factor_b.shape[1]
    axes = ("node", "local")
    device_count = lax.axis_size("node") * lax.axis_size("local")
    me = lax.axis_index("node") * lax.axis_size("local") + lax.axis_index("local")
    group_size = device_count // GROUPS
    slot_most = 2 * (5 * tok_rows // 8) // group_size
    f32, bf16 = jnp.float32, jnp.bfloat16
    experts = jnp.repeat(group_picks, 2, axis=1) * group_size + route_ids
    expert_flat = experts.reshape(-1)
    first_t = factor_a[0].T
    second = factor_b[0]
    table = jnp.zeros((rank, tok_rows), bf16).at[:topk].set(experts.T.astype(bf16))
    ids = jnp.arange(device_count, dtype=jnp.int32)
    member = (experts[:, :, None] == ids[None, None, :]).any(axis=1)
    order = jnp.cumsum(member.astype(jnp.int32), axis=0) - 1
    ranks = jnp.sum(jnp.where(experts[:, :, None] == ids, order[:, None, :], 0), axis=2)
    target = experts * slot_most + ranks
    scaled = scale_routes(grads, route_weights)
    slots = jnp.arange(device_count * slot_most, dtype=jnp.int32)
    pack = (target.reshape(1, -1) == slots[:, None]).astype(bf16)
    send_g = jnp.dot(pack, scaled, preferred_element_type=f32).astype(bf16)
    send_g = send_g.reshape(device_count, slot_most, hidden)
    own = jnp.concatenate([first_t, second, table], axis=1)
    shared = gather_shards(own, device_count)
    all_first = shared[:, :width]
    all_second = shared[:, width : width + hidden]
    tables = shared[:, width + hidden :].reshape(device_count, rank, tok_rows)[:, :topk]

    owner_mask = expert_flat[:, None] == jnp.repeat(ids, rank)[None, :]
    middle = lax.dot_general(scaled, all_second, (((1,), (1,)), ((), ())), preferred_element_type=f32)
    middle = jnp.where(owner_mask, middle, 0.0).reshape(tok_rows, topk, -1).sum(axis=1).astype(bf16)
    projected = lax.dot_general(
        tokens, all_first, (((1,), (1,)), ((), ())), preferred_element_type=f32
    ).astype(bf16)
    projected = jnp.where(
        owner_mask.reshape(tok_rows, topk, -1), projected[:, None, :], jnp.zeros((), bf16)
    ).reshape(tok_rows * topk, -1)
    share_a = lax.dot_general(middle, tokens, (((0,), (0,)), ((), ())), preferred_element_type=f32)
    share_b = lax.dot_general(projected, scaled, (((0,), (0,)), ((), ())), preferred_element_type=f32)
    half = rank // 2
    share_b = share_b.astype(bf16).reshape(device_count, 2, half, hidden)
    share_b = jnp.concatenate([share_b[:, 0], share_b[:, 1]], axis=2)
    share_b = jnp.pad(share_b, ((0, 0), (0, 0), (0, width - 2 * hidden)))
    extra = jnp.concatenate(
        [share_a.astype(bf16).reshape(device_count, rank, width), share_b], axis=1
    ).reshape(2, device_count // 4, 2, rank + half, width)

    mine = (tables == me.astype(bf16)).any(axis=1)
    place = jnp.cumsum(mine.astype(jnp.int32), axis=1) - 1
    unpack = (
        mine[:, :, None] & (place[:, :, None] == jnp.arange(slot_most, dtype=jnp.int32))
    ).astype(bf16)
    input_grad, factor_sums = return_sums(
        send_g, unpack, frozen_up[0], factor_a[0] * adapter_scale_factor, second, extra, tok_rows
    )
    factor_sums = factor_sums * (weight_gradient_total * adapter_scale_factor)
    grad_a = factor_sums[:rank].T[None]
    last = factor_sums[rank:]
    grad_b = jnp.concatenate([last[:, :hidden], last[:, hidden : 2 * hidden]], axis=0)[None]
    return (input_grad, grad_a, grad_b)


def body(tokens, grads, route_weights, route_ids, group_picks, frozen_up, factor_a, factor_b):
    tok_rows = tokens.shape[0]
    group_size = lax.axis_size("node") * lax.axis_size("local") // GROUPS
    slot_most = 2 * (5 * tok_rows // 8) // group_size
    plan = dense_body if tok_rows <= 2 * slot_most else sparse_body
    return plan(tokens, grads, route_weights, route_ids, group_picks, frozen_up, factor_a, factor_b)


def solution(mesh):
    return jax.shard_map(
        body,
        mesh=mesh,
        in_specs=(
            P(("rep", "node", "local"), None),
            P(("rep", "node", "local"), None, None),
            P(("rep", "node", "local"), None),
            P(("rep", "node", "local"), None),
            P(("rep", "node", "local"), None),
            P(("node", "local"), None, None),
            P(("node", "local"), None, None),
            P(("node", "local"), None, None),
        ),
        out_specs=(
            P(("rep", "node", "local"), None),
            P(("rep", "node", "local"), None, None),
            P(("rep", "node", "local"), None, None),
        ),
        check_vma=False,
    )
```

```python
import functools
import jax
import jax.numpy as jnp
from jax import lax
from jax.experimental import pallas as pl
from jax.experimental.pallas import tpu as pltpu
from jax.sharding import PartitionSpec as P

GROUPS = 8


adapter_scale_factor = 0.25
weight_gradient_total = 1.0 / 32.0


def slot_ranks(expert_flat, device_count):
    onehot = (expert_flat[:, None] == jnp.arange(device_count, dtype=jnp.int32)[None, :]).astype(
        jnp.int32
    )
    earlier = jnp.cumsum(onehot, axis=0) - onehot
    return jnp.sum(earlier * onehot, axis=1)


def slot_grads(arrived, arrived_grads, frozen, first, second):
    lead = arrived.shape[:-1]
    input_rows = arrived.reshape(-1, arrived.shape[-1])
    gradient_rows = arrived_grads.reshape(-1, arrived_grads.shape[-1])
    rank_space_rows = lax.dot_general(
        gradient_rows, second, (((1,), (1,)), ((), ())), preferred_element_type=jnp.float32
    ).astype(jnp.bfloat16)
    joined_rows = jnp.concatenate([gradient_rows, rank_space_rows], axis=1)
    joined_weight = jnp.concatenate([frozen, first * adapter_scale_factor], axis=1)
    route_gradient = lax.dot_general(
        joined_rows, joined_weight, (((1,), (1,)), ((), ())), preferred_element_type=jnp.float32
    ).astype(jnp.bfloat16)
    projected_rows = jnp.dot(input_rows, first, preferred_element_type=jnp.float32).astype(
        jnp.bfloat16
    )
    return (
        route_gradient.reshape(lead + (frozen.shape[0],)),
        rank_space_rows.reshape(lead + (second.shape[0],)),
        projected_rows.reshape(lead + (second.shape[0],)),
    )


def send_buffers(tokens, scaled, target, device_count, slot_most):
    tok_rows, width = tokens.shape
    pair_count, hidden = scaled.shape
    topk = pair_count // tok_rows
    scaled_pad = jnp.concatenate([scaled, jnp.zeros((1, hidden), jnp.bfloat16)], axis=0)
    tokens_pad = jnp.concatenate([tokens, jnp.zeros((1, width), jnp.bfloat16)], axis=0)
    source = jnp.full((device_count * slot_most,), pair_count, jnp.int32)
    source = source.at[target].set(jnp.arange(pair_count, dtype=jnp.int32))
    owner = jnp.where(source < pair_count, source // topk, tok_rows)
    send_x = tokens_pad[owner].reshape(device_count, slot_most, width)
    send_g = scaled_pad[source].reshape(device_count, slot_most, hidden)
    return (send_x, send_g)


def sparse_body(tokens, grads, route_weights, route_ids, group_picks, frozen_up, factor_a, factor_b):
    tok_rows = tokens.shape[0]
    topk = route_ids.shape[1]
    width = tokens.shape[1]
    hidden = grads.shape[2]
    node_count = lax.axis_size("node")
    local_count = lax.axis_size("local")
    device_count = node_count * local_count
    group_size = device_count // GROUPS
    slot_most = 2 * (5 * tok_rows // 8) // group_size
    pair_count = tok_rows * topk
    frozen = frozen_up[0]
    first = factor_a[0]
    second = factor_b[0]
    experts = jnp.repeat(group_picks, 2, axis=1) * group_size + route_ids
    expert_flat = experts.reshape(-1)
    ranks = slot_ranks(expert_flat, device_count)
    target = expert_flat * slot_most + ranks
    scaled = (
        (grads.astype(jnp.float32) * route_weights[:, :, None])
        .astype(jnp.bfloat16)
        .reshape(pair_count, hidden)
    )
    send_x, send_g = send_buffers(tokens, scaled, target, device_count, slot_most)
    pieces = (
        lax.all_to_all(send_x, ("node", "local"), split_axis=0, concat_axis=0, tiled=True),
        lax.all_to_all(send_g, ("node", "local"), split_axis=0, concat_axis=0, tiled=True),
    )
    route_gradient, rank_space_rows, projected_rows = slot_grads(
        pieces[0], pieces[1], frozen, first, second
    )
    arrived, arrived_grads, route_gradient, rank_space_rows, projected_rows = (
        pieces[0],
        pieces[1],
        route_gradient,
        rank_space_rows,
        projected_rows,
    )
    input_rows = arrived.reshape(-1, width)
    gradient_rows = arrived_grads.reshape(-1, hidden)
    first_factor_gradient = (
        weight_gradient_total
        * adapter_scale_factor
        * lax.dot_general(
            input_rows,
            rank_space_rows.reshape(-1, rank_space_rows.shape[-1]),
            (((0,), (0,)), ((), ())),
            preferred_element_type=jnp.float32,
        )
    )
    second_factor_gradient = (
        weight_gradient_total
        * adapter_scale_factor
        * lax.dot_general(
            projected_rows.reshape(-1, projected_rows.shape[-1]),
            gradient_rows,
            (((0,), (0,)), ((), ())),
            preferred_element_type=jnp.float32,
        )
    )
    returned = lax.all_to_all(
        route_gradient, ("node", "local"), split_axis=0, concat_axis=0, tiled=True
    )
    picked = returned.reshape(-1, width)[target]
    input_grad = jnp.sum(picked.reshape(tok_rows, topk, width).astype(jnp.float32), axis=1).astype(
        jnp.bfloat16
    )
    return (input_grad, first_factor_gradient[None], second_factor_gradient[None])


MESH = pl.DeviceIdType.MESH


def tile_of(width):
    for tile in (512, 256, 128):
        if width % tile == 0:
            return tile
    return width


def visit_order(count):
    table = []
    for z in range(count):
        above, below = list(range(count - 1, z, -1)), list(range(z))
        order = []
        while above or below:
            first, other = (above, below) if len(above) >= len(below) else (below, above)
            order.append(first.pop(0))
            if other:
                order.append(other.pop(0))
        table.append(order + [z])
    return table


def return_kernel(
    z_count, send_ref, unpack_ref, frozen_ref, first_ref, second_ref, extra_ref,
    out_ref, fac_ref,
    arrived, part, summed, from_y, from_z, lhs, low,
    a_send, a_recv, extra_sem, c_send, c_recv, y_send, y_recv, z_send, z_recv,
):
    f32, bf16 = jnp.float32, jnp.bfloat16
    core = lax.axis_index("node")
    local = lax.axis_index("local")
    z, y = local // 2, lax.rem(local, 2)
    tok_rows = out_ref.shape[0]
    more = fac_ref.shape[0]
    width = out_ref.shape[1]
    tile = tile_of(width)
    nt = (((1,), (1,)), ((), ()))
    table = visit_order(z_count)

    core_peer = {"node": 1 - core}
    y_peer = {"local": z * 2 + 1 - y}

    device_count = 4 * z_count
    me = core * 2 * z_count + local
    barrier = pltpu.get_barrier_semaphore()

    @pl.loop(1, device_count)
    def _(step):
        flat = lax.rem(me + step, device_count)
        peer = {"node": flat // (2 * z_count), "local": lax.rem(flat, 2 * z_count)}
        pl.semaphore_signal(barrier, inc=1, device_id=peer, device_id_type=MESH)

    target = []
    for p in range(z_count):
        zt = jnp.int32(0)
        for i in range(z_count):
            zt = zt + jnp.where(z == i, table[i][p], 0)
        target.append(zt)

    extra_copies = []
    for p in range(z_count):
        copy = pltpu.make_async_copy(
            extra_ref.at[:, target[p]],
            part.at[target[p], :, :, pl.ds(tok_rows, more)],
            extra_sem.at[p],
        )
        copy.start()
        extra_copies.append(copy)

    def partner(p, i):
        other_core = core if i // 2 == 0 else 1 - core
        other_local = target[p] * 2 + (y if i % 2 == 0 else 1 - y)
        return other_core, other_local, other_core * 2 * z_count + other_local

    def a_copy(p, i):
        other_core, other_local, flat = partner(p, i)
        return pltpu.make_async_remote_copy(
            send_ref.at[flat], arrived.at[me], a_send.at[flat], a_recv.at[me],
            device_id={"node": other_core, "local": other_local}, device_id_type=MESH,
        )

    def a_arrival(p, i):
        _, _, flat = partner(p, i)
        return pltpu.make_async_remote_copy(
            send_ref.at[flat], arrived.at[flat], a_send.at[flat], a_recv.at[flat],
            device_id=core_peer, device_id_type=MESH,
        )

    own_rows = pltpu.make_async_copy(send_ref.at[me], arrived.at[me], a_recv.at[me])
    own_rows.start()
    exchanged = [(p, i) for p in range(z_count) for i in range(4) if (p, i) != (z_count - 1, 0)]
    pl.semaphore_wait(barrier, device_count - 1)
    for p, i in exchanged:
        a_copy(p, i).start()

    def compute(p):
        zt = target[p]
        for i in range(4):
            if (p, i) in exchanged:
                a_arrival(p, i).wait_recv()
            else:
                own_rows.wait()
        for i in range(4):
            origin = (i // 2) * 2 * z_count + zt * 2 + i % 2
            rows = jnp.dot(unpack_ref[origin], arrived[origin], preferred_element_type=f32)
            lhs[pl.ds(i * tok_rows, tok_rows), :] = rows.astype(bf16)
        low[...] = lax.dot_general(
            lhs[...], second_ref[...], nt, preferred_element_type=f32
        ).astype(bf16)

        @pl.loop(0, width // tile)
        def _(j):
            columns = pl.ds(pl.multiple_of(j * tile, tile), tile)
            value = lax.dot_general(
                lhs[...], frozen_ref[columns, :], nt, preferred_element_type=f32
            ) + lax.dot_general(low[...], first_ref[columns, :], nt, preferred_element_type=f32)
            value = value.astype(bf16)
            for i in range(4):
                part[zt, i // 2, i % 2, pl.ds(0, tok_rows), columns] = value[
                    i * tok_rows : (i + 1) * tok_rows
                ]

        extra_copies[p].wait()

    def c_copy(p):
        return pltpu.make_async_remote_copy(
            part.at[target[p], 1 - core], summed.at[target[p]], c_send.at[p], c_recv.at[p],
            device_id=core_peer, device_id_type=MESH,
        )

    def y_copy(p):
        return pltpu.make_async_remote_copy(
            summed.at[target[p], 1 - y], from_y.at[target[p]], y_send.at[p], y_recv.at[p],
            device_id=y_peer, device_id_type=MESH,
        )

    def over_rows(count, step):
        @pl.loop(0, count // 16)
        def _(i):
            step(pl.ds(pl.multiple_of(i * 16, 16), 16))

    def add_core(p):
        zt = target[p]
        c_copy(p).wait_recv()
        for half in (1 - y, y):

            def step(rows):
                summed[zt, half, rows, :] = (
                    summed[zt, half, rows, :].astype(f32) + part[zt, core, half, rows, :].astype(f32)
                ).astype(bf16)

            over_rows(tok_rows + more, step)
            if half is not y:
                y_copy(p).start()

    compute(0)
    c_copy(0).start()
    for p in range(1, z_count):
        compute(p)
        c_copy(p).start()
        add_core(p - 1)
    add_core(z_count - 1)

    def z_copy(p, slot, peer):
        return pltpu.make_async_remote_copy(
            summed.at[target[p], y], from_z.at[slot], z_send.at[p], z_recv.at[slot],
            device_id={"local": peer}, device_id_type=MESH,
        )

    def slot_wait(slot):
        z_copy(0, slot, local).wait_recv()

    for p in range(z_count - 1):
        zt = target[p]
        up = zt > z
        y_copy(p).wait_recv()
        passing = jnp.logical_or(jnp.logical_and(up, z > 0), jnp.logical_and(zt < z, z < z_count - 1))

        @pl.when(passing)
        def _():
            slot_wait(zt)

            def step(rows):
                summed[zt, y, rows, :] = (
                    summed[zt, y, rows, :].astype(f32)
                    + from_y[zt, rows, :].astype(f32)
                    + from_z[zt, rows, :].astype(f32)
                ).astype(bf16)

            over_rows(tok_rows + more, step)

        @pl.when(jnp.logical_not(passing))
        def _():
            def step(rows):
                summed[zt, y, rows, :] = (
                    summed[zt, y, rows, :].astype(f32) + from_y[zt, rows, :].astype(f32)
                ).astype(bf16)

            over_rows(tok_rows + more, step)

        slot = jnp.where(zt == z - 1, z_count, zt)
        z_copy(p, slot, jnp.where(up, local + 2, local - 2)).start()

    p = z_count - 1
    y_copy(p).wait_recv()

    def finish(with_below, with_above):
        def total(rows):
            value = summed[z, y, rows, :].astype(f32) + from_y[z, rows, :].astype(f32)
            if with_below:
                value = value + from_z[z, rows, :].astype(f32)
            if with_above:
                value = value + from_z[z_count, rows, :].astype(f32)
            return value

        if with_below:
            slot_wait(z)
        if with_above:
            slot_wait(z_count)

        def step(rows):
            out_ref[rows, :] = total(rows).astype(bf16)

        over_rows(tok_rows, step)
        for start in range(0, more, 16):
            fac_ref[pl.ds(start, 16), :] = total(pl.ds(tok_rows + start, 16))

    @pl.when(z == 0)
    def _():
        finish(False, True)

    @pl.when(z == z_count - 1)
    def _():
        finish(True, False)

    @pl.when(jnp.logical_and(z > 0, z < z_count - 1))
    def _():
        finish(True, True)

    for p, i in exchanged:
        a_copy(p, i).wait_send()
    for p in range(z_count):
        c_copy(p).wait_send()
        y_copy(p).wait_send()
    for p in range(z_count - 1):
        z_copy(p, 0, local).wait_send()


def return_sums(send_g, unpack, frozen, first, second, extra, tok_rows):
    bf16 = jnp.bfloat16
    z_count, more, width = extra.shape[1], extra.shape[3], extra.shape[4]
    rows = tok_rows + more
    dma = pltpu.SemaphoreType.DMA
    vmem = pl.BlockSpec(memory_space=pltpu.VMEM)
    routes = 4 * z_count * tok_rows
    return pl.pallas_call(
        functools.partial(return_kernel, z_count),
        out_shape=(
            jax.ShapeDtypeStruct((tok_rows, width), bf16),
            jax.ShapeDtypeStruct((more, width), jnp.float32),
        ),
        in_specs=[pl.BlockSpec(memory_space=pl.ANY)] + [vmem] * 4 + [pl.BlockSpec(memory_space=pl.ANY)],
        out_specs=(vmem, vmem),
        scratch_shapes=[
            pltpu.VMEM(send_g.shape, bf16),
            pltpu.VMEM((z_count, 2, 2, rows, width), bf16),
            pltpu.VMEM((z_count, 2, rows, width), bf16),
            pltpu.VMEM((z_count, rows, width), bf16),
            pltpu.VMEM((z_count + 1, rows, width), bf16),
            pltpu.VMEM((4 * tok_rows, frozen.shape[1]), bf16),
            pltpu.VMEM((4 * tok_rows, second.shape[0]), bf16),
            dma((4 * z_count,)), dma((4 * z_count,)),
            dma((z_count,)), dma((z_count,)), dma((z_count,)), dma((z_count,)),
            dma((z_count,)), dma((z_count,)), dma((z_count + 1,)),
        ],
        compiler_params=pltpu.CompilerParams(
            collective_id=0, has_side_effects=True, vmem_limit_bytes=60 * 2**20
        ),
        cost_estimate=pl.CostEstimate(
            flops=2 * routes * width * frozen.shape[1], bytes_accessed=20 * 2**20, transcendentals=0
        ),
    )(send_g, unpack, frozen, first, second, extra)


def gather_kernel(
    z_count, own_ref, pack_ref, scaled_ref, all_ref, rows_ref, own_sem, recv, up_send, down_send, y_send, c_send
):
    core = lax.axis_index("node")
    local = lax.axis_index("local")
    z, y = local // 2, lax.rem(local, 2)
    core_peer = {"node": 1 - core}
    y_peer = {"local": z * 2 + 1 - y}
    above, below = {"local": local + 2}, {"local": local - 2}
    has_above, has_below = z < z_count - 1, z > 0

    barrier = pltpu.get_barrier_semaphore()
    pl.semaphore_signal(barrier, inc=1, device_id=core_peer, device_id_type=MESH)
    pl.semaphore_signal(barrier, inc=1, device_id=y_peer, device_id_type=MESH)

    @pl.when(has_below)
    def _():
        pl.semaphore_signal(barrier, inc=1, device_id=below, device_id_type=MESH)

    @pl.when(has_above)
    def _():
        pl.semaphore_signal(barrier, inc=1, device_id=above, device_id_type=MESH)

    place = pltpu.make_async_copy(own_ref, all_ref.at[core, z, y], own_sem)
    place.start()
    place.wait()
    neighbours = 2 + jnp.where(has_below, 1, 0) + jnp.where(has_above, 1, 0)
    pl.semaphore_wait(barrier, neighbours)

    def copy(zs, ys, send_sem, peer):
        return pltpu.make_async_remote_copy(
            all_ref.at[core, zs, ys], all_ref.at[core, zs, ys], send_sem, recv.at[core, zs, ys],
            device_id=peer, device_id_type=MESH,
        )

    def arrival(cs, zs, ys):
        pltpu.make_async_remote_copy(
            all_ref.at[cs, zs, ys], all_ref.at[cs, zs, ys], own_sem, recv.at[cs, zs, ys],
            device_id=core_peer, device_id_type=MESH,
        ).wait_recv()

    def spread(zs):
        copy(zs, y, y_send.at[zs], y_peer).start()
        copy(zs, y, c_send.at[zs, y], core_peer).start()

    @pl.when(has_above)
    def _():
        copy(z, y, up_send.at[z], above).start()

    @pl.when(has_below)
    def _():
        copy(z, y, down_send.at[z], below).start()

    spread(z)
    for distance in range(1, z_count):

        @pl.when(z - distance >= 0)
        def _():
            zs = z - distance
            arrival(core, zs, y)

            @pl.when(has_above)
            def _():
                copy(zs, y, up_send.at[zs], above).start()

            spread(zs)

        @pl.when(z + distance < z_count)
        def _():
            zs = z + distance
            arrival(core, zs, y)

            @pl.when(has_below)
            def _():
                copy(zs, y, down_send.at[zs], below).start()

            spread(zs)

    @pl.loop(0, rows_ref.shape[0])
    def _(i):
        rows_ref[i] = jnp.dot(
            pack_ref[i], scaled_ref[...], preferred_element_type=jnp.float32
        ).astype(rows_ref.dtype)

    def from_y(zs):
        arrival(core, zs, 1 - y)
        copy(zs, 1 - y, c_send.at[zs, 1 - y], core_peer).start()

    from_y(z)
    for distance in range(1, z_count):

        @pl.when(z - distance >= 0)
        def _():
            from_y(z - distance)

        @pl.when(z + distance < z_count)
        def _():
            from_y(z + distance)

    for zs in range(z_count):
        for ys in range(2):
            arrival(1 - core, zs, ys)
            copy(zs, ys, c_send.at[zs, ys], core_peer).wait_send()
        copy(zs, y, y_send.at[zs], y_peer).wait_send()

        @pl.when(jnp.logical_and(has_above, zs <= z))
        def _():
            copy(zs, y, up_send.at[zs], core_peer).wait_send()

        @pl.when(jnp.logical_and(has_below, zs >= z))
        def _():
            copy(zs, y, down_send.at[zs], core_peer).wait_send()


def gather_shards(own, pack, scaled, device_count):
    z_count = device_count // 4
    dma = pltpu.SemaphoreType.DMA
    vmem = pl.BlockSpec(memory_space=pltpu.VMEM)
    gathered, rows = pl.pallas_call(
        functools.partial(gather_kernel, z_count),
        out_shape=(
            jax.ShapeDtypeStruct((2, z_count, 2) + own.shape, own.dtype),
            jax.ShapeDtypeStruct(pack.shape[:2] + scaled.shape[1:], scaled.dtype),
        ),
        in_specs=[vmem] * 3,
        out_specs=(vmem, vmem),
        scratch_shapes=[
            dma, dma((2, z_count, 2)), dma((z_count,)), dma((z_count,)),
            dma((z_count,)), dma((z_count, 2)),
        ],
        compiler_params=pltpu.CompilerParams(
            collective_id=1, has_side_effects=True, vmem_limit_bytes=40 * 2**20
        ),
        cost_estimate=pl.CostEstimate(flops=0, bytes_accessed=100 * 2**20, transcendentals=0),
    )(own, pack, scaled)
    return gathered.reshape((device_count * own.shape[0],) + own.shape[1:]), rows


def scale_routes(grads, route_weights):
    pair_count = grads.shape[0] * grads.shape[1]
    return (
        (grads.astype(jnp.float32) * route_weights[:, :, None])
        .astype(jnp.bfloat16)
        .reshape(pair_count, grads.shape[2])
    )


def dense_body(tokens, grads, route_weights, route_ids, group_picks, frozen_up, factor_a, factor_b):
    tok_rows, width = tokens.shape
    topk = route_ids.shape[1]
    hidden = grads.shape[2]
    rank = factor_b.shape[1]
    axes = ("node", "local")
    device_count = lax.axis_size("node") * lax.axis_size("local")
    me = lax.axis_index("node") * lax.axis_size("local") + lax.axis_index("local")
    group_size = device_count // GROUPS
    slot_most = 2 * (5 * tok_rows // 8) // group_size
    f32, bf16 = jnp.float32, jnp.bfloat16
    experts = jnp.repeat(group_picks, 2, axis=1) * group_size + route_ids
    expert_flat = experts.reshape(-1)
    first_t = factor_a[0].T
    second = factor_b[0]
    table = jnp.zeros((rank, tok_rows), bf16).at[:topk].set(experts.T.astype(bf16))
    ids = jnp.arange(device_count, dtype=jnp.int32)
    member = (experts[:, :, None] == ids[None, None, :]).any(axis=1)
    order = jnp.cumsum(member.astype(jnp.int32), axis=0) - 1
    ranks = jnp.sum(jnp.where(experts[:, :, None] == ids, order[:, None, :], 0), axis=2)
    target = experts * slot_most + ranks
    scaled = scale_routes(grads, route_weights)
    slots = jnp.arange(device_count * slot_most, dtype=jnp.int32)
    pack = (target.reshape(1, -1) == slots[:, None]).astype(bf16)
    pack = pack.reshape(device_count, slot_most, -1)
    own = jnp.concatenate([first_t, second, table], axis=1)
    shared, send_g = gather_shards(own, pack, scaled, device_count)
    all_first = shared[:, :width]
    all_second = shared[:, width : width + hidden]
    tables = shared[:, width + hidden :].reshape(device_count, rank, tok_rows)[:, :topk]

    owner_mask = expert_flat[:, None] == jnp.repeat(ids, rank)[None, :]
    middle = lax.dot_general(scaled, all_second, (((1,), (1,)), ((), ())), preferred_element_type=f32)
    middle = jnp.where(owner_mask, middle, 0.0).reshape(tok_rows, topk, -1).sum(axis=1).astype(bf16)
    projected = lax.dot_general(
        tokens, all_first, (((1,), (1,)), ((), ())), preferred_element_type=f32
    ).astype(bf16)
    projected = jnp.where(
        owner_mask.reshape(tok_rows, topk, -1), projected[:, None, :], jnp.zeros((), bf16)
    ).reshape(tok_rows * topk, -1)
    share_a = lax.dot_general(middle, tokens, (((0,), (0,)), ((), ())), preferred_element_type=f32)
    share_b = lax.dot_general(projected, scaled, (((0,), (0,)), ((), ())), preferred_element_type=f32)
    half = rank // 2
    share_b = share_b.astype(bf16).reshape(device_count, 2, half, hidden)
    share_b = jnp.concatenate([share_b[:, 0], share_b[:, 1]], axis=2)
    share_b = jnp.pad(share_b, ((0, 0), (0, 0), (0, width - 2 * hidden)))
    extra = jnp.concatenate(
        [share_a.astype(bf16).reshape(device_count, rank, width), share_b], axis=1
    ).reshape(2, device_count // 4, 2, rank + half, width)

    mine = (tables == me.astype(bf16)).any(axis=1)
    place = jnp.cumsum(mine.astype(jnp.int32), axis=1) - 1
    unpack = (
        mine[:, :, None] & (place[:, :, None] == jnp.arange(slot_most, dtype=jnp.int32))
    ).astype(bf16)
    input_grad, factor_sums = return_sums(
        send_g, unpack, frozen_up[0], factor_a[0] * adapter_scale_factor, second, extra, tok_rows
    )
    factor_sums = factor_sums * (weight_gradient_total * adapter_scale_factor)
    grad_a = factor_sums[:rank].T[None]
    last = factor_sums[rank:]
    grad_b = jnp.concatenate([last[:, :hidden], last[:, hidden : 2 * hidden]], axis=0)[None]
    return (input_grad, grad_a, grad_b)


def body(tokens, grads, route_weights, route_ids, group_picks, frozen_up, factor_a, factor_b):
    tok_rows = tokens.shape[0]
    group_size = lax.axis_size("node") * lax.axis_size("local") // GROUPS
    slot_most = 2 * (5 * tok_rows // 8) // group_size
    plan = dense_body if tok_rows <= 2 * slot_most else sparse_body
    return plan(tokens, grads, route_weights, route_ids, group_picks, frozen_up, factor_a, factor_b)


def solution(mesh):
    return jax.shard_map(
        body,
        mesh=mesh,
        in_specs=(
            P(("rep", "node", "local"), None),
            P(("rep", "node", "local"), None, None),
            P(("rep", "node", "local"), None),
            P(("rep", "node", "local"), None),
            P(("rep", "node", "local"), None),
            P(("node", "local"), None, None),
            P(("node", "local"), None, None),
            P(("node", "local"), None, None),
        ),
        out_specs=(
            P(("rep", "node", "local"), None),
            P(("rep", "node", "local"), None, None),
            P(("rep", "node", "local"), None, None),
        ),
        check_vma=False,
    )
```
